1024 devices in a mesh: row: 64 (over y, x_hi, core), col: 16 (over x_lo, z).
Axes of the slice: x: 8 (x_hi: 4, x_lo: 2; x = x_hi * 2 + x_lo), y: 8, z: 8, core: 2. Of those that a mesh axis runs over, the one named last changes fastest.
Arguments:
- images: bfloat16 [24576, 1536], P('row'), may hold values from -8 to 8
- texts: bfloat16 [24576, 1536], P(('col', 'row')), may hold values from -8 to 8
- logit_scale: float32 [1], replicated, may hold values from 1.5 to 3
Outputs:
- loss_terms: float32 [24576], P(('row', 'col'))
- image_grad: float32 [24576, 1536], P(('row', 'col'))
The draws below stay inside these ranges and needn't reach their ends.
All inputs are finite; a program needn't handle non-finite values.
Results may differ from the reference program's by a relative error of at most 0.0034.
Values may be sent and summed in bfloat16 or wider, within the bound.
A program may use at most 32 MiB of HBM per device.

```python
import math
import jax
import jax.numpy as jnp
from jax import lax

D = 1536
PAIR_DEV = 24
PAIRS = 24576
N_ROW = 64
N_COL = 16


def draw_images(key, part):
    key = jax.random.fold_in(key, 1)
    values = jnp.clip(jax.random.normal(key, (PAIRS, D), jnp.float32), -6.0, 6.0)
    return values.astype(jnp.bfloat16)


def draw_texts(key, part):
    key = jax.random.fold_in(key, 2)
    values = jnp.clip(jax.random.normal(key, (PAIRS, D), jnp.float32), -6.0, 6.0)
    return values.astype(jnp.bfloat16)


def setup_inputs(seed: int = 0) -> dict:
    streams_of = jax.random.split(jax.random.key(seed), 4)
    return {
        "images": draw_images(jax.random.fold_in(streams_of[3], 71), 0),
        "texts": draw_texts(jax.random.fold_in(streams_of[3], 71), 0),
        "logit_scale": jnp.clip(jnp.exp(jax.random.uniform(streams_of[2], (1,), jnp.float32, math.log(1.5), math.log(3.0))), 1.5, 3.0),
    }


def reference(images, texts, logit_scale):
    factor = logit_scale[0] / math.sqrt(D)
    block_rows = N_COL * PAIR_DEV

    def one_block(block_index):
        first_row = (block_index * block_rows).astype(jnp.int32)
        image_rows = lax.dynamic_slice_in_dim(images, first_row, block_rows, 0)
        scores = jnp.dot(image_rows, texts.T, preferred_element_type=jnp.float32) * factor
        local_peak = lax.optimization_barrier(jnp.max(scores, axis=1))
        log_total = local_peak + jnp.log(lax.optimization_barrier(jnp.sum(jnp.exp(scores - local_peak[:, None]), axis=1)))
        positive = jnp.diagonal(lax.dynamic_slice_in_dim(scores, first_row, block_rows, 1))
        weights = jnp.exp(scores - log_total[:, None]).astype(jnp.bfloat16)
        paired = lax.dynamic_slice_in_dim(texts, first_row, block_rows, 0).astype(jnp.float32)
        grad_block = jnp.dot(weights, texts, preferred_element_type=jnp.float32) - paired
        return (log_total - positive, grad_block)
    losses, grads = lax.map(one_block, jnp.arange(N_ROW, dtype=jnp.int32))
    return (losses.reshape(-1), grads.reshape(-1, D))
```

```python
import functools
import math

import jax
import jax.numpy as jnp
from jax import lax
from jax.experimental import pallas as pl
from jax.experimental.pallas import tpu as pltpu
from jax.sharding import PartitionSpec

MESH = pl.DeviceIdType.MESH
F32 = jnp.float32
BF16 = jnp.bfloat16
LANES = 128
WIDE = 256


def nt_dot(a, b):
    return lax.dot_general(a, b, (((1,), (1,)), ((), ())), preferred_element_type=F32)


def diagonal_mask(n, lanes):
    return lax.broadcasted_iota(jnp.int32, (n, lanes), 0) == lax.broadcasted_iota(
        jnp.int32, (n, lanes), 1
    )


def to_row(spread):
    n = spread.shape[0]
    step = min(LANES, n)
    mask = diagonal_mask(step, step)
    parts = [
        jnp.sum(jnp.where(mask, spread[i : i + step, :step], 0.0), axis=0, keepdims=True)
        for i in range(0, n, step)
    ]
    return jnp.concatenate(parts, axis=1) if len(parts) > 1 else parts[0]


def to_spread(row):
    n = row.shape[1]
    step = min(LANES, n)
    mask = diagonal_mask(step, step)
    parts = []
    for i in range(0, n, step):
        piece = jnp.broadcast_to(row[:, i : i + step], (step, step))
        column = jnp.sum(jnp.where(mask, piece, 0.0), axis=1, keepdims=True)
        parts.append(jnp.broadcast_to(column, (step, LANES)))
    return jnp.concatenate(parts, axis=0) if len(parts) > 1 else parts[0]


def kernel(
    shape,
    images_hbm,
    texts_ref,
    scale_ref,
    loss_ref,
    grad_ref,
    images,
    mine_f32,
    other_f32,
    pair_out,
    pair_in,
    paired,
    gathered,
    scores,
    weights,
    peak,
    total,
    stats,
    share_me,
    share_peer,
    logs,
    own_part,
    x_out,
    x_in,
    pair_sum,
    z_out,
    z_in,
    image_sem,
    swap_sem,
    paired_sem,
    xs,
    xr,
    ys,
    yr,
    cs,
    cr,
    ss,
    sr,
    hs,
    hr,
    zs,
    zr,
):
    n_y, n_xh, n_xl, n_z, width, own, text_step = shape
    half_width = width // 2
    rows, cols = n_y * n_xh * 2, n_xl * n_z
    block = 2 * own
    n_img = own * cols
    n_half = n_img // 2
    n_wide = width // WIDE
    r, c = lax.axis_index("row"), lax.axis_index("col")
    core = r % 2
    xh = (r // 2) % n_xh
    y = r // (2 * n_xh)
    xl = c // n_z
    z = c % n_z
    factor = scale_ref[0] * (1.0 / math.sqrt(width))
    factor2 = factor * math.log2(math.e)

    def at(y_, xh_, core_):
        return ((y_ * n_xh + xh_) * 2 + core_, c)

    other_core = at(y, xh, 1 - core)
    x_peer = [at(y, (xh + d) % n_xh, core) for d in range(n_xh)]
    y_peer = [at((y + 1) % n_y, xh, core), at((y + n_y - 1) % n_y, xh, core)]
    half_peer = (r, (1 - xl) * n_z + z)
    held_text = c * rows + r
    pair_target = (held_text // cols, held_text % cols)
    held_image = r * cols + c
    pair_source = (held_image % rows, held_image // rows)
    fixed = jnp.logical_and(pair_target[0] == r, pair_target[1] == c)

    load_images = pltpu.make_async_copy(images_hbm, images, image_sem)
    load_images.start()

    barrier = pltpu.get_barrier_semaphore()

    def greet(device):
        pl.semaphore_signal(barrier, inc=1, device_id=device, device_id_type=MESH)

    greet(other_core)
    for d in range(1, n_xh):
        greet(x_peer[d])
    for d in range(2):
        greet(y_peer[d])
    for d in range(1, cols):
        greet((r, (c + d) % cols))

    @pl.when(jnp.logical_not(fixed))
    def _():
        greet(pair_source)

    held = texts_ref[...].astype(F32)
    left, right = held[:, :half_width], held[:, half_width:]
    own_rows = pl.ds(pl.multiple_of(core * own, 8), own)
    mine_f32[own_rows, :] = jnp.where(core == 0, left, right)
    other_f32[...] = jnp.where(core == 0, right, left)
    pair_out[...] = jnp.concatenate([left, right], axis=0).astype(BF16)

    pl.semaphore_wait(barrier, cols + n_xh + 1 + jnp.where(fixed, 0, 1))

    swap = pltpu.make_async_remote_copy(
        src_ref=other_f32,
        dst_ref=mine_f32.at[own_rows, :],
        send_sem=swap_sem.at[0],
        recv_sem=swap_sem.at[1],
        device_id=other_core,
        device_id_type=MESH,
    )
    swap.start()
    pair_copy = pltpu.make_async_remote_copy(
        src_ref=pair_out,
        dst_ref=pair_in,
        send_sem=paired_sem.at[0],
        recv_sem=paired_sem.at[1],
        device_id=pair_target,
        device_id_type=MESH,
    )
    pair_local = pltpu.make_async_copy(pair_out, pair_in, paired_sem.at[2])

    last = n_y // 2

    def group(way, s):
        return 0 if s == 0 else (n_y - 1 if s == last else 2 * s - 1 + way)

    def slot(g, k):
        return gathered.at[core, pl.ds((g * n_xh + k) * block, block), :]

    def x_copy(d):
        return pltpu.make_async_remote_copy(
            src_ref=slot(0, 0),
            dst_ref=slot(0, d),
            send_sem=xs.at[d],
            recv_sem=xr.at[d],
            device_id=x_peer[d],
            device_id_type=MESH,
        )

    def y_copy(way, s, k):
        return pltpu.make_async_remote_copy(
            src_ref=slot(group(way, s), k),
            dst_ref=slot(group(way, s + 1), k),
            send_sem=ys.at[way, s, k],
            recv_sem=yr.at[way, s, k],
            device_id=y_peer[way],
            device_id_type=MESH,
        )

    def goes(way, s, k):
        return s < last - 1 or (s == last - 1 and (k < n_xh // 2) == (way == 0))

    group_rows = n_xh * block

    def core_copy(g):
        place = gathered.at[core, pl.ds(g * group_rows, group_rows), :]
        return pltpu.make_async_remote_copy(
            src_ref=place,
            dst_ref=place,
            send_sem=cs.at[g],
            recv_sem=cr.at[g],
            device_id=other_core,
            device_id_type=MESH,
        )

    def score_steps(lo, hi):
        def step(i, carry):
            part = pl.ds(pl.multiple_of(i * text_step, text_step), text_step)
            scores[:, part] = nt_dot(images[:, :half_width], gathered[0, part, :]) + nt_dot(
                images[:, half_width:], gathered[1, part, :]
            )
            return carry

        if hi > lo:
            lax.fori_loop(lo, hi, step, 0)

    swap.wait()
    gathered[core, 0:block, :] = mine_f32[...].astype(BF16)
    order = [k for k in (1, n_xh - 1) if 0 < k] + list(range(2, n_xh - 1))
    order = list(dict.fromkeys(order))
    for d in order:
        x_copy(d).start()
    for way in range(2):
        y_copy(way, 0, 0).start()
    for k in order:
        x_copy(k).wait_recv()
        for way in range(2):
            if goes(way, 0, k):
                y_copy(way, 0, k).start()
    core_copy(0).start()

    @pl.when(jnp.logical_not(fixed))
    def _():
        pair_copy.start()

    @pl.when(fixed)
    def _():
        pair_local.start()

    load_images.wait()
    done = 0
    ready = []
    for s in range(1, last + 1):
        for k in [0] + order:
            for way in range(2):
                if goes(way, s - 1, k):
                    y_copy(way, s - 1, k).wait_recv()
                    if s < last and goes(way, s, k):
                        y_copy(way, s, k).start()
        new = sorted({group(0, s), group(1, s)})
        for g in new:
            core_copy(g).start()
        for g in ([0] if s == 1 else sorted({group(0, s - 1), group(1, s - 1)})):
            core_copy(g).wait_recv()
            ready.append(g)
        upto = len(ready) * group_rows // text_step
        score_steps(done, upto)
        done = upto
    core_copy(n_y - 1).wait_recv()
    score_steps(done, rows * own // text_step)

    chunk = 64 if n_img % 64 == 0 else n_img

    def soften(i, carry):
        part = pl.ds(pl.multiple_of(i * chunk, chunk), chunk)
        value = scores[part, :]
        top = jnp.max(value, axis=1, keepdims=True)
        power = jnp.exp2((value - top) * factor2)
        weights[part, :] = power.astype(BF16)
        peak[part, :] = jnp.broadcast_to(top, (chunk, LANES))
        total[part, :] = jnp.broadcast_to(jnp.sum(power, axis=1, keepdims=True), (chunk, LANES))
        return carry

    lax.fori_loop(0, n_img // chunk, soften, 0)
    stats[c] = jnp.concatenate([to_row(peak[...]), to_row(total[...])], axis=1)

    def stat_copy(d):
        return pltpu.make_async_remote_copy(
            src_ref=stats.at[c],
            dst_ref=stats.at[c],
            send_sem=ss.at[d],
            recv_sem=sr.at[d],
            device_id=(r, (c + d) % cols),
            device_id_type=MESH,
        )

    def send_stats(d, carry):
        stat_copy(d).start()
        return carry

    lax.fori_loop(1, cols, send_stats, 0)

    def half_copy(i):
        return pltpu.make_async_remote_copy(
            src_ref=x_out.at[i],
            dst_ref=x_in.at[i],
            send_sem=hs.at[i],
            recv_sem=hr.at[i],
            device_id=half_peer,
            device_id_type=MESH,
        )

    inverse = 1.0 / total[...]
    total[...] = inverse
    per_half = half_width // WIDE

    def partial(i, carry):
        columns = pl.ds(pl.multiple_of((i % per_half) * WIDE, WIDE), WIDE)
        value = jnp.dot(
            weights[...], gathered[i // per_half, :, columns], preferred_element_type=F32
        )
        scale = total[...]
        value = value * jnp.concatenate([scale, scale], axis=1)
        low, high = value[:n_half], value[n_half:]
        x_out[i] = jnp.where(xl == 0, high, low).astype(BF16)
        half_copy(i).start()
        own_part[i] = jnp.where(xl == 0, low, high)
        return carry

    lax.fori_loop(0, n_wide, partial, 0)

    def wait_stats(d, carry):
        pltpu.make_async_remote_copy(
            src_ref=stats.at[c],
            dst_ref=stats.at[(c + cols - d) % cols],
            send_sem=ss.at[d],
            recv_sem=sr.at[d],
            device_id=(r, (c + d) % cols),
            device_id_type=MESH,
        ).wait_recv()
        return carry

    lax.fori_loop(1, cols, wait_stats, 0)
    all_peak = stats[0][:, :n_img]
    for i in range(1, cols):
        all_peak = jnp.maximum(all_peak, stats[i][:, :n_img])

    def portion(value):
        return value[:, n_img:] * jnp.exp2((value[:, :n_img] - all_peak) * factor2)

    all_total = portion(stats[0])
    for i in range(1, cols):
        all_total = all_total + portion(stats[i])
    share_me[...] = to_spread(portion(stats[c]) / all_total)
    share_peer[...] = to_spread(portion(stats[half_peer[1]]) / all_total)
    logs[...] = to_spread(all_peak * factor + jnp.log(all_total))

    half_rows = pl.ds(pl.multiple_of(xl * n_half, 8), n_half)

    def z_copy(i, d):
        return pltpu.make_async_remote_copy(
            src_ref=z_out.at[i, d],
            dst_ref=z_in.at[i, d],
            send_sem=zs.at[i, d],
            recv_sem=zr.at[i, d],
            device_id=(r, xl * n_z + (z + d) % n_z),
            device_id_type=MESH,
        )

    def join(i, carry):
        half_copy(i).wait_recv()
        me, peer = share_me[half_rows, :], share_peer[half_rows, :]
        pair_sum[i] = own_part[i] * jnp.concatenate([me, me], axis=1) + x_in[i].astype(
            F32
        ) * jnp.concatenate([peer, peer], axis=1)
        for d in range(1, n_z):
            piece = pair_sum[i, pl.ds(pl.multiple_of(((z + d) % n_z) * own, 8), own), :]
            z_out[i, d] = jnp.concatenate([piece[:, :LANES], piece[:, LANES:]], axis=0).astype(BF16)
            z_copy(i, d).start()
        return carry

    lax.fori_loop(0, n_wide, join, 0)

    @pl.when(jnp.logical_not(fixed))
    def _():
        pair_copy.wait()

    @pl.when(fixed)
    def _():
        pair_local.wait()

    folded = pair_in[...].astype(F32)
    paired[...] = jnp.concatenate([folded[:own], folded[own:]], axis=1)
    near = images[pl.ds(pl.multiple_of(16 * ((own * c) // 16), 16), own + 8), :].astype(F32)
    near = jnp.where((own * c) % 16 == 0, near[:own], near[8:])
    positive = jnp.sum(near * paired[...], axis=1, keepdims=True) * factor
    own_logs = logs[pl.ds(pl.multiple_of(c * own, 8), own), :]
    loss_ref[...] = to_row(own_logs - positive)

    def finish(i, carry):
        value = pair_sum[i, pl.ds(pl.multiple_of(z * own, 8), own), :]
        for d in range(1, n_z):
            z_copy(i, d).wait_recv()
            piece = z_in[i, d].astype(F32)
            value = value + jnp.concatenate([piece[:own], piece[own:]], axis=1)
        columns = pl.ds(pl.multiple_of(i * WIDE, WIDE), WIDE)
        grad_ref[:, columns] = value - paired[:, columns]
        return carry

    lax.fori_loop(0, n_wide, finish, 0)

    for d in order:
        x_copy(d).wait_send()
    for way in range(2):
        for s in range(last):
            for k in range(n_xh):
                if goes(way, s, k):
                    y_copy(way, s, k).wait_send()
    for g in range(n_y):
        core_copy(g).wait_send()

    def wait_stat_sends(d, carry):
        stat_copy(d).wait_send()
        return carry

    lax.fori_loop(1, cols, wait_stat_sends, 0)

    def wait_sends(i, carry):
        half_copy(i).wait_send()
        for d in range(1, n_z):
            z_copy(i, d).wait_send()
        return carry

    lax.fori_loop(0, n_wide, wait_sends, 0)


def per_device(n_xh, n_xl, text_step, images, texts, logit_scale):
    own, width = texts.shape
    rows, cols = lax.axis_size("row"), lax.axis_size("col")
    n_y = rows // (2 * n_xh)
    n_z = cols // n_xl
    n_img = images.shape[0]
    n_text = rows * own
    n_wide = width // WIDE
    shape = (n_y, n_xh, n_xl, n_z, width, own, text_step)
    dma = pltpu.SemaphoreType.DMA
    vmem = pltpu.VMEM
    loss, grad = pl.pallas_call(
        functools.partial(kernel, shape),
        out_shape=(
            jax.ShapeDtypeStruct((1, own), F32),
            jax.ShapeDtypeStruct((own, width), F32),
        ),
        in_specs=[
            pl.BlockSpec(memory_space=pl.ANY),
            pl.BlockSpec(memory_space=pltpu.VMEM),
            pl.BlockSpec(memory_space=pltpu.SMEM),
        ],
        out_specs=(
            pl.BlockSpec(memory_space=pltpu.VMEM),
            pl.BlockSpec(memory_space=pltpu.VMEM),
        ),
        scratch_shapes=[
            vmem((n_img, width), BF16),
            vmem((2 * own, width // 2), F32),
            vmem((own, width // 2), F32),
            vmem((2 * own, width // 2), BF16),
            vmem((2 * own, width // 2), BF16),
            vmem((own, width), F32),
            vmem((2, n_text, width // 2), BF16),
            vmem((n_img, n_text), F32),
            vmem((n_img, n_text), BF16),
            vmem((n_img, LANES), F32),
            vmem((n_img, LANES), F32),
            vmem((cols, 1, 2 * n_img), F32),
            vmem((n_img, LANES), F32),
            vmem((n_img, LANES), F32),
            vmem((n_img, LANES), F32),
            vmem((n_wide, n_img // 2, WIDE), F32),
            vmem((n_wide, n_img // 2, WIDE), BF16),
            vmem((n_wide, n_img // 2, WIDE), BF16),
            vmem((n_wide, n_img // 2, WIDE), F32),
            vmem((n_wide, n_z, 2 * own, WIDE // 2), BF16),
            vmem((n_wide, n_z, 2 * own, WIDE // 2), BF16),
            dma(()),
            dma((2,)),
            dma((3,)),
            dma((n_xh,)),
            dma((n_xh,)),
            dma((2, n_y // 2, n_xh)),
            dma((2, n_y // 2, n_xh)),
            dma((n_y,)),
            dma((n_y,)),
            dma((cols,)),
            dma((cols,)),
            dma((n_wide,)),
            dma((n_wide,)),
            dma((n_wide, n_z)),
            dma((n_wide, n_z)),
        ],
        compiler_params=pltpu.CompilerParams(
            collective_id=0, has_side_effects=True, vmem_limit_bytes=40 * 1024 * 1024
        ),
        cost_estimate=pl.CostEstimate(
            flops=4 * n_img * n_text * width,
            bytes_accessed=2 * n_img * width,
            transcendentals=n_img * n_text,
        ),
    )(images, texts, logit_scale)
    return loss.reshape(own), grad


def solution(mesh, n_xh=4, n_xl=2, text_step=256):
    placed = (
        PartitionSpec("row", None),
        PartitionSpec(("col", "row"), None),
        PartitionSpec(),
    )
    return jax.shard_map(
        functools.partial(per_device, n_xh, n_xl, text_step),
        mesh=mesh,
        in_specs=placed,
        out_specs=(PartitionSpec(("row", "col")), PartitionSpec(("row", "col"), None)),
        check_vma=False,
    )
```

```python
import functools
import heapq
import math

import jax
import jax.numpy as jnp
from jax import lax
from jax.experimental import pallas as pl
from jax.experimental.pallas import tpu as pltpu
from jax.sharding import PartitionSpec

MESH = pl.DeviceIdType.MESH
F32 = jnp.float32
BF16 = jnp.bfloat16
LANES = 128
WIDE = 256


def nt_dot(a, b):
    return lax.dot_general(a, b, (((1,), (1,)), ((), ())), preferred_element_type=F32)


def diagonal_mask(n, lanes):
    return lax.broadcasted_iota(jnp.int32, (n, lanes), 0) == lax.broadcasted_iota(
        jnp.int32, (n, lanes), 1
    )


def to_row(spread):
    n = spread.shape[0]
    step = min(LANES, n)
    mask = diagonal_mask(step, step)
    parts = [
        jnp.sum(jnp.where(mask, spread[i : i + step, :step], 0.0), axis=0, keepdims=True)
        for i in range(0, n, step)
    ]
    return jnp.concatenate(parts, axis=1) if len(parts) > 1 else parts[0]


def to_spread(row):
    n = row.shape[1]
    step = min(LANES, n)
    mask = diagonal_mask(step, step)
    parts = []
    for i in range(0, n, step):
        piece = jnp.broadcast_to(row[:, i : i + step], (step, step))
        column = jnp.sum(jnp.where(mask, piece, 0.0), axis=1, keepdims=True)
        parts.append(jnp.broadcast_to(column, (step, LANES)))
    return jnp.concatenate(parts, axis=0) if len(parts) > 1 else parts[0]


def arrivals(n_y, block_us):
    last = n_y // 2
    free = {}
    sent = {}
    queue = []

    def send(now, piece):
        kind = piece[0]
        if kind == "x":
            link = ("x", piece[2] % 2)
            cost = (2 / 3 if piece[1] == 0 else 1 / 3) * (2 if piece[2] < 2 else 1)
        elif kind == "a":
            link, cost = ("y", piece[1]), 2 / 3
        else:
            link, cost = ("y", piece[1]), (1 / 3 if piece[2] < last - 1 else 1 / 6)
        begin = max(now, free.get(link, 0.0))
        free[link] = begin + cost * block_us
        heapq.heappush(queue, (free[link] + 2.0, len(sent), piece))
        sent[piece] = now

    def both(kind, *rest):
        return [(kind, way) + rest for way in range(2)]

    start = [("x", 0, 0), ("x", 0, 1)] + both("b", 0) + both("a", 0, 0) + [("x", 1, 0), ("x", 1, 1)]
    for piece in start:
        send(0.0, piece)
    got, result = set(), []
    while queue:
        now, _, piece = heapq.heappop(queue)
        got.add(piece)
        then = []
        if piece[0] == "x":
            _, j, i = piece
            if i < 2:
                then.append(("x", j, i + 2))
                if j == 0:
                    then += [p for p in both("a", 0, 1 if i == 0 else 3) if a_goes(last, *p[1:])]
            elif j == 0 and ("x", 0, 5 - i) in got:
                then += [p for p in both("a", 0, 2) if a_goes(last, *p[1:])]
        elif piece[0] == "a":
            _, way, s, k = piece
            if s + 1 < last and a_goes(last, way, s + 1, k):
                then.append(("a", way, s + 1, k))
        else:
            _, way, s = piece
            if s + 1 < last:
                then.append(("b", way, s + 1))
            if s + 1 < last or ("b", 1 - way, s) in got:
                g = group_of(n_y, way, s + 1)
                then += [("x", 1 + g, 0), ("x", 1 + g, 1)]
        for p in then:
            send(now, p)
        result.append((now, piece, then))
    return start, result


def a_goes(last, way, s, k):
    return s < last - 1 or (k < 2) == (way == 0)


def group_of(n_y, way, s):
    return 0 if s == 0 else (n_y - 1 if s == n_y // 2 else 2 * s - 1 + way)


def kernel(
    shape,
    images_hbm,
    texts_hbm,
    scale_ref,
    loss_ref,
    grad_ref,
    images,
    texts,
    pair_in,
    paired,
    folded,
    gathered,
    scores,
    weights,
    peak,
    total,
    stats,
    share_me,
    share_peer,
    logs,
    own_part,
    x_out,
    x_in,
    pair_sum,
    z_out,
    z_in,
    load_sem,
    paired_sem,
    xs,
    xr,
    as_,
    ar,
    bs,
    br,
    cs,
    cr,
    ss,
    sr,
    hs,
    hr,
    zs,
    zr,
):
    n_y, n_xh, n_xl, n_z, width, own, text_step = shape
    half_width = width // 2
    rows, cols = n_y * n_xh * 2, n_xl * n_z
    block = 2 * own
    cut = block * 2 // 3
    n_img = own * cols
    n_half = n_img // 2
    n_wide = width // WIDE
    last = n_y // 2
    r, c = lax.axis_index("row"), lax.axis_index("col")
    core = r % 2
    xh = (r // 2) % n_xh
    y = r // (2 * n_xh)
    xl = c // n_z
    z = c % n_z
    factor = scale_ref[0] * (1.0 / math.sqrt(width))
    factor2 = factor * math.log2(math.e)

    def at(y_, xh_, core_):
        return ((y_ * n_xh + xh_) * 2 + core_, c)

    other_core = at(y, xh, 1 - core)
    x_peer = [at(y, (xh + 1) % n_xh, core), at(y, (xh + n_xh - 1) % n_xh, core)]
    y_peer = [at((y + 1) % n_y, xh, core), at((y + n_y - 1) % n_y, xh, core)]
    half_peer = (r, (1 - xl) * n_z + z)

    held_text = c * rows + r
    pair_target = (held_text // cols, held_text % cols)
    held_image = r * cols + c
    pair_source = (held_image % rows, held_image // rows)
    fixed = jnp.logical_and(pair_target[0] == r, pair_target[1] == c)

    load_texts = pltpu.make_async_copy(texts_hbm, texts, load_sem.at[0])
    load_texts.start()
    load_images = pltpu.make_async_copy(images_hbm, images, load_sem.at[1])
    load_images.start()

    barrier = pltpu.get_barrier_semaphore()

    def greet(device):
        pl.semaphore_signal(barrier, inc=1, device_id=device, device_id_type=MESH)

    @pl.when(jnp.logical_not(fixed))
    def _():
        greet(pair_source)

    def greet_column(d, carry):
        greet((r, (c + d) % cols))
        return carry

    lax.fori_loop(1, cols, greet_column, 0)
    for peer in x_peer + y_peer + [other_core]:
        greet(peer)

    load_texts.wait()
    held = texts[...].astype(F32)
    folded[core, 0:block, :] = jnp.concatenate(
        [held[:, :half_width], held[:, half_width:]], axis=0
    ).astype(BF16)
    pl.semaphore_wait(barrier, cols + 4 + jnp.where(fixed, 0, 1))

    def piece_at(g, k, first, columns=None):
        begin = (g * n_xh + k) * block
        part = pl.ds(begin, cut) if first else pl.ds(begin + cut, block - cut)
        if columns is None:
            return folded.at[core, part, :]
        return folded.at[core, part, pl.ds(columns * (half_width // 2), half_width // 2)]

    def push(src, dst, send_sem, recv_sem, device):
        return pltpu.make_async_remote_copy(
            src_ref=src,
            dst_ref=dst,
            send_sem=send_sem,
            recv_sem=recv_sem,
            device_id=device,
            device_id_type=MESH,
        )

    def copy_of(piece):
        if piece[0] == "x":
            _, j, i = piece
            g, first = max(j - 1, 0), j == 0
            columns = None if i < 2 else i - 2
            here = 0 if i < 2 else (1 if i == 2 else 3)
            there = (1, 3, 2, 2)[i]
            return push(
                piece_at(g, here, first, columns),
                piece_at(g, there, first, columns),
                xs.at[j, i],
                xr.at[j, i],
                x_peer[i % 2],
            )
        if piece[0] == "a":
            _, way, s, k = piece
            return push(
                piece_at(group_of(n_y, way, s), k, True),
                piece_at(group_of(n_y, way, s + 1), k, True),
                as_.at[way, s, k],
                ar.at[way, s, k],
                y_peer[way],
            )
        _, way, s = piece
        columns = None if s < last - 1 else way
        return push(
            piece_at(group_of(n_y, way, s), 0, False, columns),
            piece_at(group_of(n_y, way, s + 1), 0, False, columns),
            bs.at[way, s],
            br.at[way, s],
            y_peer[way],
        )

    group_rows = n_xh * block

    def core_copy(g):
        place = folded.at[core, pl.ds(g * group_rows, group_rows), :]
        return push(place, place, cs.at[g], cr.at[g], other_core)

    def pair_copy():
        return push(
            folded.at[core, 0:block, :], pair_in, paired_sem.at[0], paired_sem.at[1], pair_target
        )

    def pair_local():
        return pltpu.make_async_copy(folded.at[core, 0:block, :], pair_in, paired_sem.at[0])

    def send_paired():
        @pl.when(jnp.logical_not(fixed))
        def _():
            pair_copy().start()

        @pl.when(fixed)
        def _():
            pair_local().start()

    def unfold(g):
        def one(k, carry):
            begin = pl.multiple_of((g * n_xh + k) * block, block)
            part = pl.ds(begin, block)
            one_, two = folded[0, part, :].astype(F32), folded[1, part, :].astype(F32)
            gathered[0, part, :] = jnp.concatenate([one_[:own], two[:own]], axis=0).astype(BF16)
            gathered[1, part, :] = jnp.concatenate([one_[own:], two[own:]], axis=0).astype(BF16)
            return carry

        lax.fori_loop(0, n_xh, one, 0)

    def score(lo, hi):
        def step(i, carry):
            part = pl.ds(pl.multiple_of(i * text_step, text_step), text_step)
            scores[:, part] = nt_dot(images[:, :half_width], gathered[0, part, :]) + nt_dot(
                images[:, half_width:], gathered[1, part, :]
            )
            return carry

        lax.fori_loop(lo, hi, step, 0)

    start, order = arrivals(n_y, 1.6)
    for piece in start:
        copy_of(piece).start()

    missing = {g: {("x", 1 + g, i) for i in range(4)} for g in range(n_y)}
    missing[0] |= {("x", 0, i) for i in range(4)}
    for _, piece, _ in order:
        if piece[0] == "a":
            missing[group_of(n_y, piece[1], piece[2] + 1)].add(piece)
        elif piece[0] == "b":
            missing[group_of(n_y, piece[1], piece[2] + 1)].add(piece)
    load_images.wait()
    flying, ready, done = [], set(), 0

    def land(now):
        nonlocal done
        while flying and flying[0][0] <= now:
            g = flying.pop(0)[1]
            core_copy(g).wait_recv()
            unfold(g)
            ready.add(g)
            upto = done
            while (upto + 1) * text_step <= n_y * n_xh * block and all(
                g_ in ready
                for g_ in range(
                    upto * text_step // group_rows, ((upto + 1) * text_step - 1) // group_rows + 1
                )
            ):
                upto += 1
            if upto > done:
                score(done, upto)
                done = upto

    for now, piece, then in order:
        land(now)
        copy_of(piece).wait_recv()
        for p in then:
            copy_of(p).start()
        for g in range(n_y):
            if piece in missing[g]:
                missing[g].remove(piece)
                if not missing[g]:
                    core_copy(g).start()
                    flying.append((now + 3.0, g))
    land(1e9)

    chunk = 64 if n_img % 64 == 0 else n_img

    def soften(i, carry):
        part = pl.ds(pl.multiple_of(i * chunk, chunk), chunk)
        value = scores[part, :]
        top = jnp.max(value, axis=1, keepdims=True)
        power = jnp.exp2((value - top) * factor2)
        weights[part, :] = power.astype(BF16)
        peak[part, :] = jnp.broadcast_to(top, (chunk, LANES))
        total[part, :] = jnp.broadcast_to(jnp.sum(power, axis=1, keepdims=True), (chunk, LANES))
        return carry

    lax.fori_loop(0, n_img // chunk, soften, 0)
    stats[c] = jnp.concatenate([to_row(peak[...]), to_row(total[...])], axis=1)

    def stat_copy(d):
        return pltpu.make_async_remote_copy(
            src_ref=stats.at[c],
            dst_ref=stats.at[c],
            send_sem=ss.at[d],
            recv_sem=sr.at[d],
            device_id=(r, (c + d) % cols),
            device_id_type=MESH,
        )

    def send_stats(d, carry):
        stat_copy(d).start()
        return carry

    lax.fori_loop(1, cols, send_stats, 0)

    def half_copy(i):
        return pltpu.make_async_remote_copy(
            src_ref=x_out.at[i],
            dst_ref=x_in.at[i],
            send_sem=hs.at[i],
            recv_sem=hr.at[i],
            device_id=half_peer,
            device_id_type=MESH,
        )

    inverse = 1.0 / total[...]
    total[...] = inverse
    per_half = half_width // WIDE

    def partial(i, carry):
        columns = pl.ds(pl.multiple_of((i % per_half) * WIDE, WIDE), WIDE)
        value = jnp.dot(
            weights[...], gathered[i // per_half, :, columns], preferred_element_type=F32
        )
        scale = total[...]
        value = value * jnp.concatenate([scale, scale], axis=1)
        low, high = value[:n_half], value[n_half:]
        x_out[i] = jnp.where(xl == 0, high, low).astype(BF16)
        half_copy(i).start()
        own_part[i] = jnp.where(xl == 0, low, high)
        return carry

    lax.fori_loop(0, n_wide, partial, 0)
    send_paired()

    def wait_stats(d, carry):
        pltpu.make_async_remote_copy(
            src_ref=stats.at[c],
            dst_ref=stats.at[(c + cols - d) % cols],
            send_sem=ss.at[d],
            recv_sem=sr.at[d],
            device_id=(r, (c + d) % cols),
            device_id_type=MESH,
        ).wait_recv()
        return carry

    lax.fori_loop(1, cols, wait_stats, 0)
    all_peak = stats[0][:, :n_img]
    for i in range(1, cols):
        all_peak = jnp.maximum(all_peak, stats[i][:, :n_img])

    def portion(value):
        return value[:, n_img:] * jnp.exp2((value[:, :n_img] - all_peak) * factor2)

    all_total = portion(stats[0])
    for i in range(1, cols):
        all_total = all_total + portion(stats[i])
    share_me[...] = to_spread(portion(stats[c]) / all_total)
    share_peer[...] = to_spread(portion(stats[half_peer[1]]) / all_total)
    logs[...] = to_spread(all_peak * factor + jnp.log(all_total))

    half_rows = pl.ds(pl.multiple_of(xl * n_half, 8), n_half)

    def z_copy(i, d):
        return pltpu.make_async_remote_copy(
            src_ref=z_out.at[i, d],
            dst_ref=z_in.at[i, d],
            send_sem=zs.at[i, d],
            recv_sem=zr.at[i, d],
            device_id=(r, xl * n_z + (z + d) % n_z),
            device_id_type=MESH,
        )

    def join(i, carry):
        half_copy(i).wait_recv()
        me, peer = share_me[half_rows, :], share_peer[half_rows, :]
        pair_sum[i] = own_part[i] * jnp.concatenate([me, me], axis=1) + x_in[i].astype(
            F32
        ) * jnp.concatenate([peer, peer], axis=1)
        for d in range(1, n_z):
            piece = pair_sum[i, pl.ds(pl.multiple_of(((z + d) % n_z) * own, 8), own), :]
            z_out[i, d] = jnp.concatenate([piece[:, :LANES], piece[:, LANES:]], axis=0).astype(BF16)
            z_copy(i, d).start()
        return carry

    lax.fori_loop(0, n_wide, join, 0)

    @pl.when(jnp.logical_not(fixed))
    def _():
        pair_copy().wait()

    @pl.when(fixed)
    def _():
        pair_local().wait()

    block_in = pair_in[...].astype(F32)
    paired[...] = jnp.concatenate([block_in[:own], block_in[own:]], axis=1)
    near = images[pl.ds(pl.multiple_of(16 * ((own * c) // 16), 16), own + 8), :].astype(F32)
    near = jnp.where((own * c) % 16 == 0, near[:own], near[8:])
    positive = jnp.sum(near * paired[...], axis=1, keepdims=True) * factor
    own_logs = logs[pl.ds(pl.multiple_of(c * own, 8), own), :]
    loss_ref[...] = to_row(own_logs - positive)

    def finish(i, carry):
        value = pair_sum[i, pl.ds(pl.multiple_of(z * own, 8), own), :]
        for d in range(1, n_z):
            z_copy(i, d).wait_recv()
            piece = z_in[i, d].astype(F32)
            value = value + jnp.concatenate([piece[:own], piece[own:]], axis=1)
        columns = pl.ds(pl.multiple_of(i * WIDE, WIDE), WIDE)
        grad_ref[:, columns] = value - paired[:, columns]
        return carry

    lax.fori_loop(0, n_wide, finish, 0)

    for piece in start:
        copy_of(piece).wait_send()
    for _, _, then in order:
        for piece in then:
            copy_of(piece).wait_send()
    for g in range(n_y):
        core_copy(g).wait_send()

    def wait_stat_sends(d, carry):
        stat_copy(d).wait_send()
        return carry

    lax.fori_loop(1, cols, wait_stat_sends, 0)

    def wait_sends(i, carry):
        half_copy(i).wait_send()
        for d in range(1, n_z):
            z_copy(i, d).wait_send()
        return carry

    lax.fori_loop(0, n_wide, wait_sends, 0)


def per_device(n_xh, n_xl, text_step, images, texts, logit_scale):
    own, width = texts.shape
    rows, cols = lax.axis_size("row"), lax.axis_size("col")
    n_y = rows // (2 * n_xh)
    n_z = cols // n_xl
    n_img = images.shape[0]
    n_text = rows * own
    n_wide = width // WIDE
    shape = (n_y, n_xh, n_xl, n_z, width, own, text_step)
    dma = pltpu.SemaphoreType.DMA
    vmem = pltpu.VMEM
    loss, grad = pl.pallas_call(
        functools.partial(kernel, shape),
        out_shape=(
            jax.ShapeDtypeStruct((1, own), F32),
            jax.ShapeDtypeStruct((own, width), F32),
        ),
        in_specs=[
            pl.BlockSpec(memory_space=pl.ANY),
            pl.BlockSpec(memory_space=pl.ANY),
            pl.BlockSpec(memory_space=pltpu.SMEM),
        ],
        out_specs=(
            pl.BlockSpec(memory_space=pltpu.VMEM),
            pl.BlockSpec(memory_space=pltpu.VMEM),
        ),
        scratch_shapes=[
            vmem((n_img, width), BF16),
            vmem((own, width), BF16),
            vmem((2 * own, width // 2), BF16),
            vmem((own, width), F32),
            vmem((2, n_text, width // 2), BF16),
            vmem((2, n_text, width // 2), BF16),
            vmem((n_img, n_text), F32),
            vmem((n_img, n_text), BF16),
            vmem((n_img, LANES), F32),
            vmem((n_img, LANES), F32),
            vmem((cols, 1, 2 * n_img), F32),
            vmem((n_img, LANES), F32),
            vmem((n_img, LANES), F32),
            vmem((n_img, LANES), F32),
            vmem((n_wide, n_img // 2, WIDE), F32),
            vmem((n_wide, n_img // 2, WIDE), BF16),
            vmem((n_wide, n_img // 2, WIDE), BF16),
            vmem((n_wide, n_img // 2, WIDE), F32),
            vmem((n_wide, n_z, 2 * own, WIDE // 2), BF16),
            vmem((n_wide, n_z, 2 * own, WIDE // 2), BF16),
            dma((2,)),
            dma((2,)),
            dma((1 + n_y, 4)),
            dma((1 + n_y, 4)),
            dma((2, n_y // 2, n_xh)),
            dma((2, n_y // 2, n_xh)),
            dma((2, n_y // 2)),
            dma((2, n_y // 2)),
            dma((n_y,)),
            dma((n_y,)),
            dma((cols,)),
            dma((cols,)),
            dma((n_wide,)),
            dma((n_wide,)),
            dma((n_wide, n_z)),
            dma((n_wide, n_z)),
        ],
        compiler_params=pltpu.CompilerParams(
            collective_id=0, has_side_effects=True, vmem_limit_bytes=60 * 1024 * 1024
        ),
        cost_estimate=pl.CostEstimate(
            flops=4 * n_img * n_text * width,
            bytes_accessed=2 * n_img * width,
            transcendentals=n_img * n_text,
        ),
    )(images, texts, logit_scale)
    return loss.reshape(own), grad


def solution(mesh, n_xh=4, n_xl=2, text_step=256):
    placed = (
        PartitionSpec("row", None),
        PartitionSpec(("col", "row"), None),
        PartitionSpec(),
    )
    return jax.shard_map(
        functools.partial(per_device, n_xh, n_xl, text_step),
        mesh=mesh,
        in_specs=placed,
        out_specs=(PartitionSpec(("row", "col")), PartitionSpec(("row", "col"), None)),
        check_vma=False,
    )
```

```python
import functools
import heapq
import math

import jax
import jax.numpy as jnp
from jax import lax
from jax.experimental import pallas as pl
from jax.experimental.pallas import tpu as pltpu
from jax.sharding import PartitionSpec

MESH = pl.DeviceIdType.MESH
F32 = jnp.float32
BF16 = jnp.bfloat16
LANES = 128
WIDE = 256


def nt_dot(a, b):
    return lax.dot_general(a, b, (((1,), (1,)), ((), ())), preferred_element_type=F32)


def diagonal_mask(n, lanes):
    return lax.broadcasted_iota(jnp.int32, (n, lanes), 0) == lax.broadcasted_iota(
        jnp.int32, (n, lanes), 1
    )


def to_row(spread):
    n = spread.shape[0]
    step = min(LANES, n)
    mask = diagonal_mask(step, step)
    parts = [
        jnp.sum(jnp.where(mask, spread[i : i + step, :step], 0.0), axis=0, keepdims=True)
        for i in range(0, n, step)
    ]
    return jnp.concatenate(parts, axis=1) if len(parts) > 1 else parts[0]


def to_spread(row):
    n = row.shape[1]
    step = min(LANES, n)
    mask = diagonal_mask(step, step)
    parts = []
    for i in range(0, n, step):
        piece = jnp.broadcast_to(row[:, i : i + step], (step, step))
        column = jnp.sum(jnp.where(mask, piece, 0.0), axis=1, keepdims=True)
        parts.append(jnp.broadcast_to(column, (step, LANES)))
    return jnp.concatenate(parts, axis=0) if len(parts) > 1 else parts[0]


def origin(last, piece):
    if piece[0] == "b":
        return (0, piece[2] + 1) if piece[2] + 1 < last else (last - 1, 1)
    d = piece[2] + 1
    if piece[3] == 2 and d > 1:
        return (0, 2) if d == 2 else (2, d - 2)
    return (d - 1, 1)


def a_goes(last, way, s, k):
    return s < last - 1 or (k % 2 == 0) == (way == 0)


def arrivals(n_y, block_us, latency):
    last = n_y // 2
    free = {}
    queue = []

    def along_y(kind, way, d, *k):
        pieces = [(kind, way, s) + k for s in range(last)]
        return [
            p
            for p in pieces
            if origin(last, p)[0] == d and (kind == "b" or a_goes(last, *p[1:]))
        ]

    def both(kind, d, *k):
        return along_y(kind, 0, d, *k) + along_y(kind, 1, d, *k)

    def send(now, piece):
        if piece[0] == "x":
            link = ("x", piece[2] % 2)
            hops = 2
            cost = (2 / 3 if piece[1] == 0 else 1 / 3) * (2 if piece[2] < 2 else 1)
        else:
            link = ("y", piece[1])
            hops = origin(last, piece)[1]
            cost = hops * (2 / 3 if piece[0] == "a" else (1 / 3 if piece[2] < last - 1 else 1 / 6))
        free[link] = max(now, free.get(link, 0.0)) + cost * block_us
        heapq.heappush(queue, (free[link] + latency + 0.3 * (hops - 1), len(sent), piece))
        sent.append(piece)

    sent = []
    start = [("x", 0, 0), ("x", 0, 1)] + both("a", 0, 0) + both("b", 0) + [("x", 1, 0), ("x", 1, 1)]
    for piece in start:
        send(0.0, piece)
    got, result, clock = set(), [], 0.0
    while queue:
        now, _, piece = heapq.heappop(queue)
        clock = max(now, clock + 0.05)
        got.add(piece)
        then = []
        if piece[0] == "x":
            _, j, i = piece
            if i < 2:
                if j == 0:
                    then += both("a", 0, 1 if i == 0 else 3)
                then.append(("x", j, i + 2))
            elif j == 0 and ("x", 0, 5 - i) in got:
                then += both("a", 0, 2)
        elif piece[0] == "a":
            _, way, s, k = piece
            then += along_y("a", way, s + 1, k)
        else:
            _, way, s = piece
            then += along_y("b", way, s + 1)
            if s + 1 < last or ("b", 1 - way, s) in got:
                g = group_of(n_y, way, s + 1)
                then += [("x", 1 + g, 0), ("x", 1 + g, 1)]
        for p in then:
            send(clock, p)
        result.append((clock, piece, then))
    return start, result


def group_of(n_y, way, s):
    return 0 if s == 0 else (n_y - 1 if s == n_y // 2 else 2 * s - 1 + way)


def kernel(
    shape,
    images_hbm,
    texts_hbm,
    scale_ref,
    loss_ref,
    grad_ref,
    images,
    texts,
    pair_in,
    relay,
    paired,
    folded,
    gathered,
    scores,
    weights,
    peak,
    total,
    stats,
    share_me,
    share_peer,
    logs,
    own_part,
    x_out,
    x_in,
    pair_sum,
    z_out,
    z_in,
    load_sem,
    paired_sem,
    ps,
    xs,
    xr,
    as_,
    ar,
    bs,
    br,
    cs,
    cr,
    ss,
    sr,
    hs,
    hr,
    zs,
    zr,
):
    n_y, n_xh, n_xl, n_z, width, own, text_step = shape
    half_width = width // 2
    rows, cols = n_y * n_xh * 2, n_xl * n_z
    block = 2 * own
    cut = block * 2 // 3
    n_img = own * cols
    n_half = n_img // 2
    n_wide = width // WIDE
    last = n_y // 2
    r, c = lax.axis_index("row"), lax.axis_index("col")
    core = r % 2
    xh = (r // 2) % n_xh
    y = r // (2 * n_xh)
    xl = c // n_z
    z = c % n_z
    factor = scale_ref[0] * (1.0 / math.sqrt(width))
    factor2 = factor * math.log2(math.e)

    def at(y_, xh_, core_):
        return ((y_ * n_xh + xh_) * 2 + core_, c)

    other_core = at(y, xh, 1 - core)
    x_peer = [at(y, (xh + 1) % n_xh, core), at(y, (xh + n_xh - 1) % n_xh, core)]

    def y_peer(way, hops):
        return at((y + (hops if way == 0 else n_y - hops)) % n_y, xh, core)

    half_peer = (r, (1 - xl) * n_z + z)

    held_image = r * cols + c
    pair_col = ((r // 2) * 2 * cols) // rows
    pair_source = ((r // 2) * 2 + (held_image % rows) % 2, pair_col)
    near_side = pair_col // n_z == xl
    aligned = pair_col == c
    fixed = jnp.logical_and(pair_source[0] == r, aligned)
    near_other = jnp.logical_and(near_side, jnp.logical_not(fixed))

    load_texts = pltpu.make_async_copy(texts_hbm, texts, load_sem.at[0])
    load_texts.start()
    load_images = pltpu.make_async_copy(images_hbm, images, load_sem.at[1])
    load_images.start()

    barrier = pltpu.get_barrier_semaphore()

    def greet(device):
        pl.semaphore_signal(barrier, inc=1, device_id=device, device_id_type=MESH)

    @pl.when(near_other)
    def _():
        greet(pair_source)

    def greet_column(d, carry):
        greet((r, (c + d) % cols))
        return carry

    lax.fori_loop(1, cols, greet_column, 0)
    for peer in [y_peer(0, hops) for hops in range(1, n_y)] + x_peer + [other_core]:
        greet(peer)

    load_texts.wait()
    held = texts[...].astype(F32)
    folded[core, 0:block, :] = jnp.concatenate(
        [held[:, :half_width], held[:, half_width:]], axis=0
    ).astype(BF16)
    pl.semaphore_wait(barrier, cols + n_y + 1 + jnp.where(aligned, n_z, 0) - jnp.where(fixed, 1, 0))

    def piece_at(g, k, first, columns=None):
        begin = (g * n_xh + k) * block
        part = pl.ds(begin, cut) if first else pl.ds(begin + cut, block - cut)
        if columns is None:
            return folded.at[core, part, :]
        return folded.at[core, part, pl.ds(columns * (half_width // 2), half_width // 2)]

    def push(src, dst, send_sem, recv_sem, device):
        return pltpu.make_async_remote_copy(
            src_ref=src,
            dst_ref=dst,
            send_sem=send_sem,
            recv_sem=recv_sem,
            device_id=device,
            device_id_type=MESH,
        )

    def copy_of(piece):
        if piece[0] == "x":
            _, j, i = piece
            g, first = max(j - 1, 0), j == 0
            columns = None if i < 2 else i - 2
            here = 0 if i < 2 else (1 if i == 2 else 3)
            there = (1, 3, 2, 2)[i]
            return push(
                piece_at(g, here, first, columns),
                piece_at(g, there, first, columns),
                xs.at[j, i],
                xr.at[j, i],
                x_peer[i % 2],
            )
        if piece[0] == "a":
            _, way, s, k = piece
            return push(
                piece_at(group_of(n_y, way, origin(last, piece)[0]), k, True),
                piece_at(group_of(n_y, way, s + 1), k, True),
                as_.at[way, s, k],
                ar.at[way, s, k],
                y_peer(way, origin(last, piece)[1]),
            )
        _, way, s = piece
        columns = None if s < last - 1 else way
        return push(
            piece_at(group_of(n_y, way, origin(last, piece)[0]), 0, False, columns),
            piece_at(group_of(n_y, way, s + 1), 0, False, columns),
            bs.at[way, s],
            br.at[way, s],
            y_peer(way, origin(last, piece)[1]),
        )

    group_rows = n_xh * block

    def core_copy(g):
        place = folded.at[core, pl.ds(g * group_rows, group_rows), :]
        return push(place, place, cs.at[g], cr.at[g], other_core)

    def pair_copies(g, act):
        step = (g + 1) // 2
        y_from = (y + (n_y - step if g % 2 == 1 else step)) % n_y

        def one(k, carry):
            text = c * rows + (y_from * n_xh + (xh + n_xh - k) % n_xh) * 2 + core
            to_r, to_c = text // cols, text % cols
            here = jnp.logical_and(to_r == r, to_c % n_z == z)
            leaves = jnp.logical_and(to_r // 2 == r // 2, jnp.logical_not(here))
            place = folded.at[core, pl.ds(pl.multiple_of((g * n_xh + k) * block, block), block), :]
            target = (to_r, xl * n_z + to_c % n_z)

            @pl.when(jnp.logical_and(leaves, to_c // n_z == xl))
            def _():
                act(push(place, pair_in, ps.at[g, k], paired_sem.at[0], target))

            @pl.when(jnp.logical_and(leaves, to_c // n_z != xl))
            def _():
                act(push(place, relay, ps.at[g, k], paired_sem.at[1], target))

            return carry

        lax.fori_loop(0, n_xh, one, 0)

    def held_place(image):
        text = image % rows
        away = (y + n_y - text // (2 * n_xh)) % n_y
        g = jnp.where(
            away == last, n_y - 1, jnp.where(away > last, 2 * (n_y - away), jnp.maximum(2 * away - 1, 0))
        )
        k = (xh + n_xh - (text // 2) % n_xh) % n_xh
        return folded.at[core, pl.ds(pl.multiple_of((g * n_xh + k) * block, block), block), :]

    def relay_copy(place):
        return push(place, pair_in, paired_sem.at[2], paired_sem.at[0], half_peer)

    def relay_paired():
        @pl.when(near_other)
        def _():
            push(relay, relay, paired_sem.at[2], paired_sem.at[1], half_peer).wait_recv()
            relay_copy(relay).start()

        @pl.when(fixed)
        def _():
            relay_copy(held_place(r * cols + half_peer[1])).start()

    def unfold(g):
        def one(k, carry):
            begin = pl.multiple_of((g * n_xh + k) * block, block)
            part = pl.ds(begin, block)
            one_, two = folded[0, part, :].astype(F32), folded[1, part, :].astype(F32)
            gathered[0, part, :] = jnp.concatenate([one_[:own], two[:own]], axis=0).astype(BF16)
            gathered[1, part, :] = jnp.concatenate([one_[own:], two[own:]], axis=0).astype(BF16)
            return carry

        lax.fori_loop(0, n_xh, one, 0)

    def score(lo, hi):
        def step(i, carry):
            part = pl.ds(pl.multiple_of(i * text_step, text_step), text_step)
            scores[:, part] = nt_dot(images[:, :half_width], gathered[0, part, :]) + nt_dot(
                images[:, half_width:], gathered[1, part, :]
            )
            return carry

        lax.fori_loop(lo, hi, step, 0)

    start, order = arrivals(n_y, 1.55, 2.9)
    for piece in start:
        copy_of(piece).start()

    missing = {g: {("x", 1 + g, i) for i in range(4)} for g in range(n_y)}
    missing[0] |= {("x", 0, i) for i in range(4)}
    for _, piece, _ in order:
        if piece[0] == "a":
            missing[group_of(n_y, piece[1], piece[2] + 1)].add(piece)
        elif piece[0] == "b":
            missing[group_of(n_y, piece[1], piece[2] + 1)].add(piece)
    load_images.wait()
    flying, ready, done = [], set(), 0

    def land(now):
        nonlocal done
        while flying and flying[0][0] <= now:
            g = flying.pop(0)[1]
            core_copy(g).wait_recv()
            unfold(g)
            ready.add(g)
            upto = done
            while (upto + 1) * text_step <= n_y * n_xh * block and all(
                g_ in ready
                for g_ in range(
                    upto * text_step // group_rows, ((upto + 1) * text_step - 1) // group_rows + 1
                )
            ):
                upto += 1
            if upto > done:
                score(done, upto)
                done = upto

    for now, piece, then in order:
        land(now)
        copy_of(piece).wait_recv()
        for p in then:
            copy_of(p).start()
        for g in range(n_y):
            if piece in missing[g]:
                missing[g].remove(piece)
                if not missing[g]:
                    core_copy(g).start()
                    pair_copies(g, lambda copy: copy.start())
                    flying.append((now + 3.0, g))
    land(1e9)

    chunk = 64 if n_img % 64 == 0 else n_img

    def soften(i, carry):
        part = pl.ds(pl.multiple_of(i * chunk, chunk), chunk)
        value = scores[part, :]
        top = jnp.max(value, axis=1, keepdims=True)
        power = jnp.exp2((value - top) * factor2)
        weights[part, :] = power.astype(BF16)
        peak[part, :] = jnp.broadcast_to(top, (chunk, LANES))
        total[part, :] = jnp.broadcast_to(jnp.sum(power, axis=1, keepdims=True), (chunk, LANES))
        return carry

    lax.fori_loop(0, n_img // chunk, soften, 0)
    stats[c] = jnp.concatenate([to_row(peak[...]), to_row(total[...])], axis=1)

    def stat_copy(d):
        return pltpu.make_async_remote_copy(
            src_ref=stats.at[c],
            dst_ref=stats.at[c],
            send_sem=ss.at[d],
            recv_sem=sr.at[d],
            device_id=(r, (c + d) % cols),
            device_id_type=MESH,
        )

    def send_stats(d, carry):
        stat_copy(d).start()
        return carry

    lax.fori_loop(1, cols, send_stats, 0)

    def half_copy(i):
        return pltpu.make_async_remote_copy(
            src_ref=x_out.at[i],
            dst_ref=x_in.at[i],
            send_sem=hs.at[i],
            recv_sem=hr.at[i],
            device_id=half_peer,
            device_id_type=MESH,
        )

    inverse = 1.0 / total[...]
    total[...] = inverse
    per_half = half_width // WIDE

    def partial(i, carry):
        columns = pl.ds(pl.multiple_of((i % per_half) * WIDE, WIDE), WIDE)
        value = jnp.dot(
            weights[...], gathered[i // per_half, :, columns], preferred_element_type=F32
        )
        scale = total[...]
        value = value * jnp.concatenate([scale, scale], axis=1)
        low, high = value[:n_half], value[n_half:]
        x_out[i] = jnp.where(xl == 0, high, low).astype(BF16)
        half_copy(i).start()
        own_part[i] = jnp.where(xl == 0, low, high)
        return carry

    lax.fori_loop(0, n_wide, partial, 0)

    def wait_stats(d, carry):
        pltpu.make_async_remote_copy(
            src_ref=stats.at[c],
            dst_ref=stats.at[(c + cols - d) % cols],
            send_sem=ss.at[d],
            recv_sem=sr.at[d],
            device_id=(r, (c + d) % cols),
            device_id_type=MESH,
        ).wait_recv()
        return carry

    lax.fori_loop(1, cols, wait_stats, 0)
    all_peak = stats[0][:, :n_img]
    for i in range(1, cols):
        all_peak = jnp.maximum(all_peak, stats[i][:, :n_img])

    def portion(value):
        return value[:, n_img:] * jnp.exp2((value[:, :n_img] - all_peak) * factor2)

    all_total = portion(stats[0])
    for i in range(1, cols):
        all_total = all_total + portion(stats[i])
    share_me[...] = to_spread(portion(stats[c]) / all_total)
    share_peer[...] = to_spread(portion(stats[half_peer[1]]) / all_total)
    logs[...] = to_spread(all_peak * factor + jnp.log(all_total))

    half_rows = pl.ds(pl.multiple_of(xl * n_half, 8), n_half)

    def z_copy(i, d):
        return pltpu.make_async_remote_copy(
            src_ref=z_out.at[i, d],
            dst_ref=z_in.at[i, d],
            send_sem=zs.at[i, d],
            recv_sem=zr.at[i, d],
            device_id=(r, xl * n_z + (z + d) % n_z),
            device_id_type=MESH,
        )

    def join(i, carry):
        half_copy(i).wait_recv()
        me, peer = share_me[half_rows, :], share_peer[half_rows, :]
        pair_sum[i] = own_part[i] * jnp.concatenate([me, me], axis=1) + x_in[i].astype(
            F32
        ) * jnp.concatenate([peer, peer], axis=1)
        for d in range(1, n_z):
            piece = pair_sum[i, pl.ds(pl.multiple_of(((z + d) % n_z) * own, 8), own), :]
            z_out[i, d] = jnp.concatenate([piece[:, :LANES], piece[:, LANES:]], axis=0).astype(BF16)
            z_copy(i, d).start()
        return carry

    relay_paired()
    lax.fori_loop(0, n_wide, join, 0)

    @pl.when(jnp.logical_not(fixed))
    def _():
        relay_copy(pair_in).wait_recv()

    @pl.when(fixed)
    def _():
        take = pltpu.make_async_copy(held_place(held_image), pair_in, paired_sem.at[3])
        take.start()
        take.wait()

    block_in = pair_in[...].astype(F32)
    paired[...] = jnp.concatenate([block_in[:own], block_in[own:]], axis=1)
    near = images[pl.ds(pl.multiple_of(16 * ((own * c) // 16), 16), own + 8), :].astype(F32)
    near = jnp.where((own * c) % 16 == 0, near[:own], near[8:])
    positive = jnp.sum(near * paired[...], axis=1, keepdims=True) * factor
    own_logs = logs[pl.ds(pl.multiple_of(c * own, 8), own), :]
    loss_ref[...] = to_row(own_logs - positive)

    def finish(i, carry):
        value = pair_sum[i, pl.ds(pl.multiple_of(z * own, 8), own), :]
        for d in range(1, n_z):
            z_copy(i, d).wait_recv()
            piece = z_in[i, d].astype(F32)
            value = value + jnp.concatenate([piece[:own], piece[own:]], axis=1)
        columns = pl.ds(pl.multiple_of(i * WIDE, WIDE), WIDE)
        grad_ref[:, columns] = value - paired[:, columns]
        return carry

    lax.fori_loop(0, n_wide, finish, 0)

    for piece in start:
        copy_of(piece).wait_send()
    for _, _, then in order:
        for piece in then:
            copy_of(piece).wait_send()
    for g in range(n_y):
        core_copy(g).wait_send()
        pair_copies(g, lambda copy: copy.wait_send())

    @pl.when(near_side)
    def _():
        relay_copy(relay).wait_send()

    def wait_stat_sends(d, carry):
        stat_copy(d).wait_send()
        return carry

    lax.fori_loop(1, cols, wait_stat_sends, 0)

    def wait_sends(i, carry):
        half_copy(i).wait_send()
        for d in range(1, n_z):
            z_copy(i, d).wait_send()
        return carry

    lax.fori_loop(0, n_wide, wait_sends, 0)


def per_device(n_xh, n_xl, text_step, images, texts, logit_scale):
    own, width = texts.shape
    rows, cols = lax.axis_size("row"), lax.axis_size("col")
    n_y = rows // (2 * n_xh)
    n_z = cols // n_xl
    n_img = images.shape[0]
    n_text = rows * own
    n_wide = width // WIDE
    shape = (n_y, n_xh, n_xl, n_z, width, own, text_step)
    dma = pltpu.SemaphoreType.DMA
    vmem = pltpu.VMEM
    loss, grad = pl.pallas_call(
        functools.partial(kernel, shape),
        out_shape=(
            jax.ShapeDtypeStruct((1, own), F32),
            jax.ShapeDtypeStruct((own, width), F32),
        ),
        in_specs=[
            pl.BlockSpec(memory_space=pl.ANY),
            pl.BlockSpec(memory_space=pl.ANY),
            pl.BlockSpec(memory_space=pltpu.SMEM),
        ],
        out_specs=(
            pl.BlockSpec(memory_space=pltpu.VMEM),
            pl.BlockSpec(memory_space=pltpu.VMEM),
        ),
        scratch_shapes=[
            vmem((n_img, width), BF16),
            vmem((own, width), BF16),
            vmem((2 * own, width // 2), BF16),
            vmem((2 * own, width // 2), BF16),
            vmem((own, width), F32),
            vmem((2, n_text, width // 2), BF16),
            vmem((2, n_text, width // 2), BF16),
            vmem((n_img, n_text), F32),
            vmem((n_img, n_text), BF16),
            vmem((n_img, LANES), F32),
            vmem((n_img, LANES), F32),
            vmem((cols, 1, 2 * n_img), F32),
            vmem((n_img, LANES), F32),
            vmem((n_img, LANES), F32),
            vmem((n_img, LANES), F32),
            vmem((n_wide, n_img // 2, WIDE), F32),
            vmem((n_wide, n_img // 2, WIDE), BF16),
            vmem((n_wide, n_img // 2, WIDE), BF16),
            vmem((n_wide, n_img // 2, WIDE), F32),
            vmem((n_wide, n_z, 2 * own, WIDE // 2), BF16),
            vmem((n_wide, n_z, 2 * own, WIDE // 2), BF16),
            dma((2,)),
            dma((4,)),
            dma((n_y, n_xh)),
            dma((1 + n_y, 4)),
            dma((1 + n_y, 4)),
            dma((2, n_y // 2, n_xh)),
            dma((2, n_y // 2, n_xh)),
            dma((2, n_y // 2)),
            dma((2, n_y // 2)),
            dma((n_y,)),
            dma((n_y,)),
            dma((cols,)),
            dma((cols,)),
            dma((n_wide,)),
            dma((n_wide,)),
            dma((n_wide, n_z)),
            dma((n_wide, n_z)),
        ],
        compiler_params=pltpu.CompilerParams(
            collective_id=0, has_side_effects=True, vmem_limit_bytes=60 * 1024 * 1024
        ),
        cost_estimate=pl.CostEstimate(
            flops=4 * n_img * n_text * width,
            bytes_accessed=2 * n_img * width,
            transcendentals=n_img * n_text,
        ),
    )(images, texts, logit_scale)
    return loss.reshape(own), grad


def solution(mesh, n_xh=4, n_xl=2, text_step=256):
    placed = (
        PartitionSpec("row", None),
        PartitionSpec(("col", "row"), None),
        PartitionSpec(),
    )
    return jax.shard_map(
        functools.partial(per_device, n_xh, n_xl, text_step),
        mesh=mesh,
        in_specs=placed,
        out_specs=(PartitionSpec(("row", "col")), PartitionSpec(("row", "col"), None)),
        check_vma=False,
    )
```

```python
import functools
import heapq
import math

import jax
import jax.numpy as jnp
from jax import lax
from jax.experimental import pallas as pl
from jax.experimental.pallas import tpu as pltpu
from jax.sharding import PartitionSpec

MESH = pl.DeviceIdType.MESH
F32 = jnp.float32
BF16 = jnp.bfloat16
LANES = 128
WIDE = 256


def nt_dot(a, b):
    return lax.dot_general(a, b, (((1,), (1,)), ((), ())), preferred_element_type=F32)


def diagonal_mask(n, lanes):
    return lax.broadcasted_iota(jnp.int32, (n, lanes), 0) == lax.broadcasted_iota(
        jnp.int32, (n, lanes), 1
    )


def to_row(spread):
    n = spread.shape[0]
    step = min(LANES, n)
    mask = diagonal_mask(step, step)
    parts = [
        jnp.sum(jnp.where(mask, spread[i : i + step, :step], 0.0), axis=0, keepdims=True)
        for i in range(0, n, step)
    ]
    return jnp.concatenate(parts, axis=1) if len(parts) > 1 else parts[0]


def to_spread(row):
    n = row.shape[1]
    step = min(LANES, n)
    mask = diagonal_mask(step, step)
    parts = []
    for i in range(0, n, step):
        piece = jnp.broadcast_to(row[:, i : i + step], (step, step))
        column = jnp.sum(jnp.where(mask, piece, 0.0), axis=1, keepdims=True)
        parts.append(jnp.broadcast_to(column, (step, LANES)))
    return jnp.concatenate(parts, axis=0) if len(parts) > 1 else parts[0]


def origin(last, piece):
    if piece[0] == "b":
        return (0, piece[2] + 1) if piece[2] + 1 < last else (last - 1, 1)
    d = piece[2] + 1
    if piece[3] == 2 and d > 1:
        return (0, 2) if d == 2 else (2, d - 2)
    return (d - 1, 1)


def a_goes(last, way, s, k):
    return s < last - 1 or (k % 2 == 0) == (way == 0)


def arrivals(n_y, block_us, latency):
    last = n_y // 2
    free = {}
    queue = []

    def along_y(kind, way, d, *k):
        pieces = [(kind, way, s) + k for s in range(last)]
        return [
            p
            for p in pieces
            if origin(last, p)[0] == d and (kind == "b" or a_goes(last, *p[1:]))
        ]

    def both(kind, d, *k):
        return along_y(kind, 0, d, *k) + along_y(kind, 1, d, *k)

    def send(now, piece):
        if piece[0] == "x":
            link = ("x", piece[2] % 2)
            hops = 2
            cost = (2 / 3 if piece[1] == 0 else 1 / 3) * (2 if piece[2] < 2 else 1)
        else:
            link = ("y", piece[1])
            hops = origin(last, piece)[1]
            cost = hops * (2 / 3 if piece[0] == "a" else (1 / 3 if piece[2] < last - 1 else 1 / 6))
        free[link] = max(now, free.get(link, 0.0)) + cost * block_us
        heapq.heappush(queue, (free[link] + latency + 0.3 * (hops - 1), len(sent), piece))
        sent.append(piece)

    sent = []
    start = [("x", 0, 0), ("x", 0, 1)] + both("a", 0, 0) + both("b", 0) + [("x", 1, 0), ("x", 1, 1)]
    for piece in start:
        send(0.0, piece)
    got, result, clock = set(), [], 0.0
    while queue:
        now, _, piece = heapq.heappop(queue)
        clock = max(now, clock + 0.05)
        got.add(piece)
        then = []
        if piece[0] == "x":
            _, j, i = piece
            if i < 2:
                if j == 0:
                    then += both("a", 0, 1 if i == 0 else 3)
                then.append(("x", j, i + 2))
            elif j == 0 and ("x", 0, 5 - i) in got:
                then += both("a", 0, 2)
        elif piece[0] == "a":
            _, way, s, k = piece
            then += along_y("a", way, s + 1, k)
        else:
            _, way, s = piece
            then += along_y("b", way, s + 1)
            if s + 1 < last or ("b", 1 - way, s) in got:
                g = group_of(n_y, way, s + 1)
                then += [("x", 1 + g, 0), ("x", 1 + g, 1)]
        for p in then:
            send(clock, p)
        result.append((clock, piece, then))
    return start, result


def group_of(n_y, way, s):
    return 0 if s == 0 else (n_y - 1 if s == n_y // 2 else 2 * s - 1 + way)


def kernel(
    shape,
    images_hbm,
    texts_hbm,
    scale_ref,
    loss_ref,
    grad_ref,
    images,
    texts,
    pair_in,
    relay,
    paired,
    folded,
    gathered,
    scores,
    weights,
    peak,
    total,
    stats,
    share_me,
    share_peer,
    logs,
    own_part,
    x_out,
    x_in,
    pair_sum,
    z_out,
    z_in,
    load_sem,
    paired_sem,
    ps,
    xs,
    xr,
    as_,
    ar,
    bs,
    br,
    cs,
    cr,
    ss,
    sr,
    hs,
    hr,
    zs,
    zr,
):
    n_y, n_xh, n_xl, n_z, width, own, text_step = shape
    half_width = width // 2
    rows, cols = n_y * n_xh * 2, n_xl * n_z
    block = 2 * own
    cut = block * 2 // 3
    n_img = own * cols
    n_half = n_img // 2
    n_wide = width // WIDE
    last = n_y // 2
    r, c = lax.axis_index("row"), lax.axis_index("col")
    core = r % 2
    xh = (r // 2) % n_xh
    y = r // (2 * n_xh)
    xl = c // n_z
    z = c % n_z
    factor = scale_ref[0] * (1.0 / math.sqrt(width))
    factor2 = factor * math.log2(math.e)

    def at(y_, xh_, core_):
        return ((y_ * n_xh + xh_) * 2 + core_, c)

    other_core = at(y, xh, 1 - core)
    x_peer = [at(y, (xh + 1) % n_xh, core), at(y, (xh + n_xh - 1) % n_xh, core)]

    def y_peer(way, hops):
        return at((y + (hops if way == 0 else n_y - hops)) % n_y, xh, core)

    half_peer = (r, (1 - xl) * n_z + z)

    held_image = r * cols + c
    pair_col = ((r // 2) * 2 * cols) // rows
    pair_source = ((r // 2) * 2 + (held_image % rows) % 2, pair_col)
    near_side = pair_col // n_z == xl
    aligned = pair_col == c
    fixed = jnp.logical_and(pair_source[0] == r, aligned)
    near_other = jnp.logical_and(near_side, jnp.logical_not(fixed))

    load_texts = pltpu.make_async_copy(texts_hbm, texts, load_sem.at[0])
    load_texts.start()
    load_images = pltpu.make_async_copy(images_hbm, images, load_sem.at[1])
    load_images.start()

    barrier = pltpu.get_barrier_semaphore()

    def greet(device):
        pl.semaphore_signal(barrier, inc=1, device_id=device, device_id_type=MESH)

    @pl.when(near_other)
    def _():
        greet(pair_source)

    def greet_column(d, carry):
        greet((r, (c + d) % cols))
        return carry

    lax.fori_loop(1, cols, greet_column, 0)
    for peer in [y_peer(0, hops) for hops in range(1, n_y)] + x_peer + [other_core]:
        greet(peer)

    load_texts.wait()
    held = texts[...].astype(F32)
    folded[core, 0:block, :] = jnp.concatenate(
        [held[:, :half_width], held[:, half_width:]], axis=0
    ).astype(BF16)
    pl.semaphore_wait(barrier, cols + n_y + 1 + jnp.where(aligned, n_z, 0) - jnp.where(fixed, 1, 0))

    def piece_at(g, k, first, columns=None):
        begin = (g * n_xh + k) * block
        part = pl.ds(begin, cut) if first else pl.ds(begin + cut, block - cut)
        if columns is None:
            return folded.at[core, part, :]
        return folded.at[core, part, pl.ds(columns * (half_width // 2), half_width // 2)]

    def push(src, dst, send_sem, recv_sem, device):
        return pltpu.make_async_remote_copy(
            src_ref=src,
            dst_ref=dst,
            send_sem=send_sem,
            recv_sem=recv_sem,
            device_id=device,
            device_id_type=MESH,
        )

    def copy_of(piece):
        if piece[0] == "x":
            _, j, i = piece
            g, first = max(j - 1, 0), j == 0
            columns = None if i < 2 else i - 2
            here = 0 if i < 2 else (1 if i == 2 else 3)
            there = (1, 3, 2, 2)[i]
            return push(
                piece_at(g, here, first, columns),
                piece_at(g, there, first, columns),
                xs.at[j, i],
                xr.at[j, i],
                x_peer[i % 2],
            )
        if piece[0] == "a":
            _, way, s, k = piece
            return push(
                piece_at(group_of(n_y, way, origin(last, piece)[0]), k, True),
                piece_at(group_of(n_y, way, s + 1), k, True),
                as_.at[way, s, k],
                ar.at[way, s, k],
                y_peer(way, origin(last, piece)[1]),
            )
        _, way, s = piece
        columns = None if s < last - 1 else way
        return push(
            piece_at(group_of(n_y, way, origin(last, piece)[0]), 0, False, columns),
            piece_at(group_of(n_y, way, s + 1), 0, False, columns),
            bs.at[way, s],
            br.at[way, s],
            y_peer(way, origin(last, piece)[1]),
        )

    group_rows = n_xh * block

    def core_copy(g):
        place = folded.at[core, pl.ds(g * group_rows, group_rows), :]
        return push(place, place, cs.at[g], cr.at[g], other_core)

    def pair_copies(g, act):
        step = (g + 1) // 2
        y_from = (y + (n_y - step if g % 2 == 1 else step)) % n_y

        def one(k, carry):
            text = c * rows + (y_from * n_xh + (xh + n_xh - k) % n_xh) * 2 + core
            to_r, to_c = text // cols, text % cols
            here = jnp.logical_and(to_r == r, to_c % n_z == z)
            leaves = jnp.logical_and(to_r // 2 == r // 2, jnp.logical_not(here))
            place = folded.at[core, pl.ds(pl.multiple_of((g * n_xh + k) * block, block), block), :]
            target = (to_r, xl * n_z + to_c % n_z)

            @pl.when(jnp.logical_and(leaves, to_c // n_z == xl))
            def _():
                act(push(place, pair_in, ps.at[g, k], paired_sem.at[0], target))

            @pl.when(jnp.logical_and(leaves, to_c // n_z != xl))
            def _():
                act(push(place, relay, ps.at[g, k], paired_sem.at[1], target))

            return carry

        lax.fori_loop(0, n_xh, one, 0)

    def held_place(image):
        text = image % rows
        away = (y + n_y - text // (2 * n_xh)) % n_y
        g = jnp.where(
            away == last, n_y - 1, jnp.where(away > last, 2 * (n_y - away), jnp.maximum(2 * away - 1, 0))
        )
        k = (xh + n_xh - (text // 2) % n_xh) % n_xh
        return folded.at[core, pl.ds(pl.multiple_of((g * n_xh + k) * block, block), block), :]

    def relay_copy(place):
        return push(place, pair_in, paired_sem.at[2], paired_sem.at[0], half_peer)

    def relay_paired():
        @pl.when(near_other)
        def _():
            push(relay, relay, paired_sem.at[2], paired_sem.at[1], half_peer).wait_recv()
            relay_copy(relay).start()

        @pl.when(fixed)
        def _():
            relay_copy(held_place(r * cols + half_peer[1])).start()

    def unfold(g):
        def one(k, carry):
            begin = pl.multiple_of((g * n_xh + k) * block, block)
            part = pl.ds(begin, block)
            one_, two = folded[0, part, :].astype(F32), folded[1, part, :].astype(F32)
            gathered[0, part, :] = jnp.concatenate([one_[:own], two[:own]], axis=0).astype(BF16)
            gathered[1, part, :] = jnp.concatenate([one_[own:], two[own:]], axis=0).astype(BF16)
            return carry

        lax.fori_loop(0, n_xh, one, 0)

    def score(lo, hi):
        def step(i, carry):
            part = pl.ds(pl.multiple_of(i * text_step, text_step), text_step)
            scores[:, part] = nt_dot(images[:, :half_width], gathered[0, part, :]) + nt_dot(
                images[:, half_width:], gathered[1, part, :]
            )
            return carry

        lax.fori_loop(lo, hi, step, 0)

    start, order = arrivals(n_y, 1.55, 2.9)
    for piece in start:
        copy_of(piece).start()

    missing = {g: {("x", 1 + g, i) for i in range(4)} for g in range(n_y)}
    missing[0] |= {("x", 0, i) for i in range(4)}
    for _, piece, _ in order:
        if piece[0] == "a":
            missing[group_of(n_y, piece[1], piece[2] + 1)].add(piece)
        elif piece[0] == "b":
            missing[group_of(n_y, piece[1], piece[2] + 1)].add(piece)
    load_images.wait()
    flying, ready, done = [], set(), 0

    def land(now):
        nonlocal done
        while flying and flying[0][0] <= now:
            g = flying.pop(0)[1]
            core_copy(g).wait_recv()
            unfold(g)
            ready.add(g)
            upto = done
            while (upto + 1) * text_step <= n_y * n_xh * block and all(
                g_ in ready
                for g_ in range(
                    upto * text_step // group_rows, ((upto + 1) * text_step - 1) // group_rows + 1
                )
            ):
                upto += 1
            if upto > done:
                score(done, upto)
                done = upto

    for now, piece, then in order:
        land(now)
        copy_of(piece).wait_recv()
        for p in then:
            copy_of(p).start()
        for g in range(n_y):
            if piece in missing[g]:
                missing[g].remove(piece)
                if not missing[g]:
                    core_copy(g).start()
                    pair_copies(g, lambda copy: copy.start())
                    flying.append((now + 3.0, g))
    land(1e9)

    chunk = 64 if n_img % 64 == 0 else n_img

    def soften(i, carry):
        part = pl.ds(pl.multiple_of(i * chunk, chunk), chunk)
        value = scores[part, :]
        top = jnp.max(value, axis=1, keepdims=True)
        power = jnp.exp2((value - top) * factor2)
        weights[part, :] = power.astype(BF16)
        peak[part, :] = jnp.broadcast_to(top, (chunk, LANES))
        total[part, :] = jnp.broadcast_to(jnp.sum(power, axis=1, keepdims=True), (chunk, LANES))
        return carry

    lax.fori_loop(0, n_img // chunk, soften, 0)
    stats[c] = jnp.concatenate([to_row(peak[...]), to_row(total[...])], axis=1)

    def stat_copy(d):
        return pltpu.make_async_remote_copy(
            src_ref=stats.at[c],
            dst_ref=stats.at[c],
            send_sem=ss.at[d],
            recv_sem=sr.at[d],
            device_id=(r, (c + d) % cols),
            device_id_type=MESH,
        )

    def send_stats(d, carry):
        stat_copy(d).start()
        return carry

    lax.fori_loop(1, cols, send_stats, 0)

    def half_copy(i):
        return pltpu.make_async_remote_copy(
            src_ref=x_out.at[i],
            dst_ref=x_in.at[i],
            send_sem=hs.at[i],
            recv_sem=hr.at[i],
            device_id=half_peer,
            device_id_type=MESH,
        )

    inverse = 1.0 / total[...]
    total[...] = inverse
    per_half = half_width // WIDE

    def partial(i, carry):
        columns = pl.ds(pl.multiple_of((i % per_half) * WIDE, WIDE), WIDE)
        value = jnp.dot(
            weights[...], gathered[i // per_half, :, columns], preferred_element_type=F32
        )
        scale = total[...]
        value = value * jnp.concatenate([scale, scale], axis=1)
        low, high = value[:n_half], value[n_half:]
        x_out[i] = jnp.where(xl == 0, high, low).astype(BF16)
        half_copy(i).start()
        own_part[i] = jnp.where(xl == 0, low, high)
        return carry

    lax.fori_loop(0, n_wide, partial, 0)

    def wait_stats(d, carry):
        pltpu.make_async_remote_copy(
            src_ref=stats.at[c],
            dst_ref=stats.at[(c + cols - d) % cols],
            send_sem=ss.at[d],
            recv_sem=sr.at[d],
            device_id=(r, (c + d) % cols),
            device_id_type=MESH,
        ).wait_recv()
        return carry

    lax.fori_loop(1, cols, wait_stats, 0)
    all_peak = stats[0][:, :n_img]
    for i in range(1, cols):
        all_peak = jnp.maximum(all_peak, stats[i][:, :n_img])

    def portion(value):
        return value[:, n_img:] * jnp.exp2((value[:, :n_img] - all_peak) * factor2)

    all_total = portion(stats[0])
    for i in range(1, cols):
        all_total = all_total + portion(stats[i])
    share_me[...] = to_spread(portion(stats[c]) / all_total)
    share_peer[...] = to_spread(portion(stats[half_peer[1]]) / all_total)
    logs[...] = to_spread(all_peak * factor + jnp.log(all_total))

    half_rows = pl.ds(pl.multiple_of(xl * n_half, 8), n_half)

    def z_copy(i, d):
        return pltpu.make_async_remote_copy(
            src_ref=z_out.at[i, d],
            dst_ref=z_in.at[i, d],
            send_sem=zs.at[i, d],
            recv_sem=zr.at[i, d],
            device_id=(r, xl * n_z + (z + d) % n_z),
            device_id_type=MESH,
        )

    def join(i, carry):
        half_copy(i).wait_recv()
        me, peer = share_me[half_rows, :], share_peer[half_rows, :]
        pair_sum[i] = own_part[i] * jnp.concatenate([me, me], axis=1) + x_in[i].astype(
            F32
        ) * jnp.concatenate([peer, peer], axis=1)
        for d in range(1, n_z):
            piece = pair_sum[i, pl.ds(pl.multiple_of(((z + d) % n_z) * own, 8), own), :]
            z_out[i, d] = jnp.concatenate([piece[:, :LANES], piece[:, LANES:]], axis=0).astype(BF16)
            z_copy(i, d).start()
        return carry

    relay_paired()
    lax.fori_loop(0, n_wide, join, 0)

    for piece in start:
        copy_of(piece).wait_send()
    for _, _, then in order:
        for piece in then:
            copy_of(piece).wait_send()
    for g in range(n_y):
        core_copy(g).wait_send()
        pair_copies(g, lambda copy: copy.wait_send())

    @pl.when(near_side)
    def _():
        relay_copy(relay).wait_send()

    def wait_stat_sends(d, carry):
        stat_copy(d).wait_send()
        return carry

    lax.fori_loop(1, cols, wait_stat_sends, 0)

    @pl.when(jnp.logical_not(fixed))
    def _():
        relay_copy(pair_in).wait_recv()

    @pl.when(fixed)
    def _():
        take = pltpu.make_async_copy(held_place(held_image), pair_in, paired_sem.at[3])
        take.start()
        take.wait()

    block_in = pair_in[...].astype(F32)
    paired[...] = jnp.concatenate([block_in[:own], block_in[own:]], axis=1)
    near = images[pl.ds(pl.multiple_of(16 * ((own * c) // 16), 16), own + 8), :].astype(F32)
    near = jnp.where((own * c) % 16 == 0, near[:own], near[8:])
    positive = jnp.sum(near * paired[...], axis=1, keepdims=True) * factor
    own_logs = logs[pl.ds(pl.multiple_of(c * own, 8), own), :]
    loss_ref[...] = to_row(own_logs - positive)

    def finish(i, carry):
        value = pair_sum[i, pl.ds(pl.multiple_of(z * own, 8), own), :]
        for d in range(1, n_z):
            z_copy(i, d).wait_recv()
            piece = z_in[i, d].astype(F32)
            value = value + jnp.concatenate([piece[:own], piece[own:]], axis=1)
        columns = pl.ds(pl.multiple_of(i * WIDE, WIDE), WIDE)
        grad_ref[:, columns] = value - paired[:, columns]
        half_copy(i).wait_send()
        for d in range(1, n_z):
            z_copy(i, d).wait_send()
        return carry

    lax.fori_loop(0, n_wide, finish, 0)


def per_device(n_xh, n_xl, text_step, images, texts, logit_scale):
    own, width = texts.shape
    rows, cols = lax.axis_size("row"), lax.axis_size("col")
    n_y = rows // (2 * n_xh)
    n_z = cols // n_xl
    n_img = images.shape[0]
    n_text = rows * own
    n_wide = width // WIDE
    shape = (n_y, n_xh, n_xl, n_z, width, own, text_step)
    dma = pltpu.SemaphoreType.DMA
    vmem = pltpu.VMEM
    loss, grad = pl.pallas_call(
        functools.partial(kernel, shape),
        out_shape=(
            jax.ShapeDtypeStruct((1, own), F32),
            jax.ShapeDtypeStruct((own, width), F32),
        ),
        in_specs=[
            pl.BlockSpec(memory_space=pl.ANY),
            pl.BlockSpec(memory_space=pl.ANY),
            pl.BlockSpec(memory_space=pltpu.SMEM),
        ],
        out_specs=(
            pl.BlockSpec(memory_space=pltpu.VMEM),
            pl.BlockSpec(memory_space=pltpu.VMEM),
        ),
        scratch_shapes=[
            vmem((n_img, width), BF16),
            vmem((own, width), BF16),
            vmem((2 * own, width // 2), BF16),
            vmem((2 * own, width // 2), BF16),
            vmem((own, width), F32),
            vmem((2, n_text, width // 2), BF16),
            vmem((2, n_text, width // 2), BF16),
            vmem((n_img, n_text), F32),
            vmem((n_img, n_text), BF16),
            vmem((n_img, LANES), F32),
            vmem((n_img, LANES), F32),
            vmem((cols, 1, 2 * n_img), F32),
            vmem((n_img, LANES), F32),
            vmem((n_img, LANES), F32),
            vmem((n_img, LANES), F32),
            vmem((n_wide, n_img // 2, WIDE), F32),
            vmem((n_wide, n_img // 2, WIDE), BF16),
            vmem((n_wide, n_img // 2, WIDE), BF16),
            vmem((n_wide, n_img // 2, WIDE), F32),
            vmem((n_wide, n_z, 2 * own, WIDE // 2), BF16),
            vmem((n_wide, n_z, 2 * own, WIDE // 2), BF16),
            dma((2,)),
            dma((4,)),
            dma((n_y, n_xh)),
            dma((1 + n_y, 4)),
            dma((1 + n_y, 4)),
            dma((2, n_y // 2, n_xh)),
            dma((2, n_y // 2, n_xh)),
            dma((2, n_y // 2)),
            dma((2, n_y // 2)),
            dma((n_y,)),
            dma((n_y,)),
            dma((cols,)),
            dma((cols,)),
            dma((n_wide,)),
            dma((n_wide,)),
            dma((n_wide, n_z)),
            dma((n_wide, n_z)),
        ],
        compiler_params=pltpu.CompilerParams(
            collective_id=0, has_side_effects=True, vmem_limit_bytes=60 * 1024 * 1024
        ),
        cost_estimate=pl.CostEstimate(
            flops=4 * n_img * n_text * width,
            bytes_accessed=2 * n_img * width,
            transcendentals=n_img * n_text,
        ),
    )(images, texts, logit_scale)
    return loss.reshape(own), grad


def solution(mesh, n_xh=4, n_xl=2, text_step=256):
    placed = (
        PartitionSpec("row", None),
        PartitionSpec(("col", "row"), None),
        PartitionSpec(),
    )
    return jax.shard_map(
        functools.partial(per_device, n_xh, n_xl, text_step),
        mesh=mesh,
        in_specs=placed,
        out_specs=(PartitionSpec(("row", "col")), PartitionSpec(("row", "col"), None)),
        check_vma=False,
    )
```

```python
import functools
import heapq
import math

import jax
import jax.numpy as jnp
from jax import lax
from jax.experimental import pallas as pl
from jax.experimental.pallas import tpu as pltpu
from jax.sharding import PartitionSpec

MESH = pl.DeviceIdType.MESH
F32 = jnp.float32
BF16 = jnp.bfloat16
LANES = 128
WIDE = 256


def nt_dot(a, b):
    return lax.dot_general(a, b, (((1,), (1,)), ((), ())), preferred_element_type=F32)


def diagonal_mask(n, lanes):
    return lax.broadcasted_iota(jnp.int32, (n, lanes), 0) == lax.broadcasted_iota(
        jnp.int32, (n, lanes), 1
    )


def to_row(spread):
    n = spread.shape[0]
    step = min(LANES, n)
    mask = diagonal_mask(step, step)
    parts = [
        jnp.sum(jnp.where(mask, spread[i : i + step, :step], 0.0), axis=0, keepdims=True)
        for i in range(0, n, step)
    ]
    return jnp.concatenate(parts, axis=1) if len(parts) > 1 else parts[0]


def to_spread(row):
    n = row.shape[1]
    step = min(LANES, n)
    mask = diagonal_mask(step, step)
    parts = []
    for i in range(0, n, step):
        piece = jnp.broadcast_to(row[:, i : i + step], (step, step))
        column = jnp.sum(jnp.where(mask, piece, 0.0), axis=1, keepdims=True)
        parts.append(jnp.broadcast_to(column, (step, LANES)))
    return jnp.concatenate(parts, axis=0) if len(parts) > 1 else parts[0]


def origin(last, piece):
    if piece[0] == "b":
        return (0, piece[2] + 1) if piece[2] + 1 < last else (last - 1, 1)
    d = piece[2] + 1
    if piece[3] == 2 and d > 1:
        return (0, 2) if d == 2 else (2, d - 2)
    return (d - 1, 1)


def a_goes(last, way, s, k):
    return s < last - 1 or (k % 2 == 0) == (way == 0)


def arrivals(n_y, block_us, latency):
    last = n_y // 2
    free = {}
    queue = []

    def along_y(kind, way, d, *k):
        pieces = [(kind, way, s) + k for s in range(last)]
        return [
            p
            for p in pieces
            if origin(last, p)[0] == d and (kind == "b" or a_goes(last, *p[1:]))
        ]

    def both(kind, d, *k):
        return along_y(kind, 0, d, *k) + along_y(kind, 1, d, *k)

    def send(now, piece):
        if piece[0] == "x":
            link = ("x", piece[2] % 2)
            hops = 2
            cost = (2 / 3 if piece[1] == 0 else 1 / 3) * (2 if piece[2] < 2 else 1)
        else:
            link = ("y", piece[1])
            hops = origin(last, piece)[1]
            cost = hops * (2 / 3 if piece[0] == "a" else (1 / 3 if piece[2] < last - 1 else 1 / 6))
        free[link] = max(now, free.get(link, 0.0)) + cost * block_us
        heapq.heappush(queue, (free[link] + latency + 0.3 * (hops - 1), len(sent), piece))
        sent.append(piece)

    sent = []
    start = [("x", 0, 0), ("x", 0, 1)] + both("a", 0, 0) + both("b", 0) + [("x", 1, 0), ("x", 1, 1)]
    for piece in start:
        send(0.0, piece)
    got, result, clock = set(), [], 0.0
    while queue:
        now, _, piece = heapq.heappop(queue)
        clock = max(now, clock + 0.05)
        got.add(piece)
        then = []
        if piece[0] == "x":
            _, j, i = piece
            if i < 2:
                if j == 0:
                    then += both("a", 0, 1 if i == 0 else 3)
                then.append(("x", j, i + 2))
            elif j == 0 and ("x", 0, 5 - i) in got:
                then += both("a", 0, 2)
        elif piece[0] == "a":
            _, way, s, k = piece
            then += along_y("a", way, s + 1, k)
        else:
            _, way, s = piece
            then += along_y("b", way, s + 1)
            if s + 1 < last or ("b", 1 - way, s) in got:
                g = group_of(n_y, way, s + 1)
                then += [("x", 1 + g, 0), ("x", 1 + g, 1)]
        for p in then:
            send(clock, p)
        result.append((clock, piece, then))
    return start, result


def group_of(n_y, way, s):
    return 0 if s == 0 else (n_y - 1 if s == n_y // 2 else 2 * s - 1 + way)


def kernel(
    shape,
    images_hbm,
    texts_hbm,
    scale_ref,
    loss_ref,
    grad_ref,
    images,
    texts,
    pair_in,
    relay,
    paired,
    folded,
    gathered,
    scores,
    weights,
    peak,
    total,
    stats,
    share_me,
    share_peer,
    logs,
    own_part,
    x_out,
    x_in,
    pair_sum,
    z_out,
    z_in,
    load_sem,
    paired_sem,
    ps,
    xs,
    xr,
    as_,
    ar,
    bs,
    br,
    cs,
    cr,
    ss,
    sr,
    hs,
    hr,
    zs,
    zr,
):
    n_y, n_xh, n_xl, n_z, width, own, text_step = shape
    half_width = width // 2
    rows, cols = n_y * n_xh * 2, n_xl * n_z
    block = 2 * own
    cut = block * 2 // 3
    n_img = own * cols
    n_half = n_img // 2
    n_wide = width // WIDE
    last = n_y // 2
    r, c = lax.axis_index("row"), lax.axis_index("col")
    core = r % 2
    xh = (r // 2) % n_xh
    y = r // (2 * n_xh)
    xl = c // n_z
    z = c % n_z
    factor = scale_ref[0] * (1.0 / math.sqrt(width))
    factor2 = factor * math.log2(math.e)

    def at(y_, xh_, core_):
        return ((y_ * n_xh + xh_) * 2 + core_, c)

    other_core = at(y, xh, 1 - core)
    x_peer = [at(y, (xh + 1) % n_xh, core), at(y, (xh + n_xh - 1) % n_xh, core)]

    def y_peer(way, hops):
        return at((y + (hops if way == 0 else n_y - hops)) % n_y, xh, core)

    half_peer = (r, (1 - xl) * n_z + z)

    held_image = r * cols + c
    pair_col = ((r // 2) * 2 * cols) // rows
    pair_source = ((r // 2) * 2 + (held_image % rows) % 2, pair_col)
    near_side = pair_col // n_z == xl
    aligned = pair_col == c
    fixed = jnp.logical_and(pair_source[0] == r, aligned)
    near_other = jnp.logical_and(near_side, jnp.logical_not(fixed))

    load_texts = pltpu.make_async_copy(texts_hbm, texts, load_sem.at[0])
    load_texts.start()
    load_images = pltpu.make_async_copy(images_hbm, images, load_sem.at[1])
    load_images.start()

    barrier = pltpu.get_barrier_semaphore()

    def greet(device):
        pl.semaphore_signal(barrier, inc=1, device_id=device, device_id_type=MESH)

    @pl.when(near_other)
    def _():
        greet(pair_source)

    def greet_column(d, carry):
        greet((r, (c + d) % cols))
        return carry

    lax.fori_loop(1, cols, greet_column, 0)
    for peer in [y_peer(0, hops) for hops in range(1, n_y)] + x_peer + [other_core]:
        greet(peer)

    load_texts.wait()
    held = texts[...].astype(F32)
    folded[core, 0:block, :] = jnp.concatenate(
        [held[:, :half_width], held[:, half_width:]], axis=0
    ).astype(BF16)
    pl.semaphore_wait(barrier, cols + n_y + 1 + jnp.where(aligned, n_z, 0) - jnp.where(fixed, 1, 0))

    def piece_at(g, k, first, columns=None):
        begin = (g * n_xh + k) * block
        part = pl.ds(begin, cut) if first else pl.ds(begin + cut, block - cut)
        if columns is None:
            return folded.at[core, part, :]
        return folded.at[core, part, pl.ds(columns * (half_width // 2), half_width // 2)]

    def push(src, dst, send_sem, recv_sem, device):
        return pltpu.make_async_remote_copy(
            src_ref=src,
            dst_ref=dst,
            send_sem=send_sem,
            recv_sem=recv_sem,
            device_id=device,
            device_id_type=MESH,
        )

    def copy_of(piece):
        if piece[0] == "x":
            _, j, i = piece
            g, first = max(j - 1, 0), j == 0
            columns = None if i < 2 else i - 2
            here = 0 if i < 2 else (1 if i == 2 else 3)
            there = (1, 3, 2, 2)[i]
            return push(
                piece_at(g, here, first, columns),
                piece_at(g, there, first, columns),
                xs.at[j, i],
                xr.at[j, i],
                x_peer[i % 2],
            )
        if piece[0] == "a":
            _, way, s, k = piece
            return push(
                piece_at(group_of(n_y, way, origin(last, piece)[0]), k, True),
                piece_at(group_of(n_y, way, s + 1), k, True),
                as_.at[way, s, k],
                ar.at[way, s, k],
                y_peer(way, origin(last, piece)[1]),
            )
        _, way, s = piece
        columns = None if s < last - 1 else way
        return push(
            piece_at(group_of(n_y, way, origin(last, piece)[0]), 0, False, columns),
            piece_at(group_of(n_y, way, s + 1), 0, False, columns),
            bs.at[way, s],
            br.at[way, s],
            y_peer(way, origin(last, piece)[1]),
        )

    group_rows = n_xh * block

    def core_copy(g):
        place = folded.at[core, pl.ds(g * group_rows, group_rows), :]
        return push(place, place, cs.at[g], cr.at[g], other_core)

    def pair_copies(g, act):
        step = (g + 1) // 2
        y_from = (y + (n_y - step if g % 2 == 1 else step)) % n_y

        def one(k, carry):
            text = c * rows + (y_from * n_xh + (xh + n_xh - k) % n_xh) * 2 + core
            to_r, to_c = text // cols, text % cols
            here = jnp.logical_and(to_r == r, to_c % n_z == z)
            leaves = jnp.logical_and(to_r // 2 == r // 2, jnp.logical_not(here))
            place = folded.at[core, pl.ds(pl.multiple_of((g * n_xh + k) * block, block), block), :]
            target = (to_r, xl * n_z + to_c % n_z)

            @pl.when(jnp.logical_and(leaves, to_c // n_z == xl))
            def _():
                act(push(place, pair_in, ps.at[g, k], paired_sem.at[0], target))

            @pl.when(jnp.logical_and(leaves, to_c // n_z != xl))
            def _():
                act(push(place, relay, ps.at[g, k], paired_sem.at[1], target))

            return carry

        lax.fori_loop(0, n_xh, one, 0)

    def held_place(image):
        text = image % rows
        away = (y + n_y - text // (2 * n_xh)) % n_y
        g = jnp.where(
            away == last, n_y - 1, jnp.where(away > last, 2 * (n_y - away), jnp.maximum(2 * away - 1, 0))
        )
        k = (xh + n_xh - (text // 2) % n_xh) % n_xh
        return folded.at[core, pl.ds(pl.multiple_of((g * n_xh + k) * block, block), block), :]

    def relay_copy(place):
        return push(place, pair_in, paired_sem.at[2], paired_sem.at[0], half_peer)

    def relay_paired():
        @pl.when(near_other)
        def _():
            push(relay, relay, paired_sem.at[2], paired_sem.at[1], half_peer).wait_recv()
            relay_copy(relay).start()

        @pl.when(fixed)
        def _():
            relay_copy(held_place(r * cols + half_peer[1])).start()

    def unfold(g):
        def one(k, carry):
            begin = pl.multiple_of((g * n_xh + k) * block, block)
            part = pl.ds(begin, block)
            one_, two = folded[0, part, :].astype(F32), folded[1, part, :].astype(F32)
            gathered[0, part, :] = jnp.concatenate([one_[:own], two[:own]], axis=0).astype(BF16)
            gathered[1, part, :] = jnp.concatenate([one_[own:], two[own:]], axis=0).astype(BF16)
            return carry

        lax.fori_loop(0, n_xh, one, 0)

    def score(lo, hi):
        def step(i, carry):
            part = pl.ds(pl.multiple_of(i * text_step, text_step), text_step)
            scores[:, part] = nt_dot(images[:, :half_width], gathered[0, part, :]) + nt_dot(
                images[:, half_width:], gathered[1, part, :]
            )
            return carry

        lax.fori_loop(lo, hi, step, 0)

    start, order = arrivals(n_y, 1.55, 2.9)
    for piece in start:
        copy_of(piece).start()

    missing = {g: {("x", 1 + g, i) for i in range(4)} for g in range(n_y)}
    missing[0] |= {("x", 0, i) for i in range(4)}
    for _, piece, _ in order:
        if piece[0] == "a":
            missing[group_of(n_y, piece[1], piece[2] + 1)].add(piece)
        elif piece[0] == "b":
            missing[group_of(n_y, piece[1], piece[2] + 1)].add(piece)
    load_images.wait()
    flying, ready, done = [], set(), 0

    def land(now):
        nonlocal done
        while flying and flying[0][0] <= now:
            g = flying.pop(0)[1]
            core_copy(g).wait_recv()
            unfold(g)
            ready.add(g)
            upto = done
            while (upto + 1) * text_step <= n_y * n_xh * block and all(
                g_ in ready
                for g_ in range(
                    upto * text_step // group_rows, ((upto + 1) * text_step - 1) // group_rows + 1
                )
            ):
                upto += 1
            if upto > done:
                score(done, upto)
                done = upto

    for now, piece, then in order:
        land(now)
        copy_of(piece).wait_recv()
        for p in then:
            copy_of(p).start()
        for g in range(n_y):
            if piece in missing[g]:
                missing[g].remove(piece)
                if not missing[g]:
                    core_copy(g).start()
                    pair_copies(g, lambda copy: copy.start())
                    flying.append((now + 3.0, g))
    land(1e9)

    chunk = 32 if n_img % 32 == 0 else n_img

    def soften(i, carry):
        part = pl.ds(pl.multiple_of(i * chunk, chunk), chunk)
        value = scores[part, :]
        top = jnp.max(value, axis=1, keepdims=True)
        power = jnp.exp2((value - top) * factor2)
        weights[part, :] = power.astype(BF16)
        peak[part, :] = jnp.broadcast_to(top, (chunk, LANES))
        total[part, :] = jnp.broadcast_to(jnp.sum(power, axis=1, keepdims=True), (chunk, LANES))
        return carry

    lax.fori_loop(0, n_img // chunk, soften, 0)
    stats[c] = jnp.concatenate([to_row(peak[...]), to_row(total[...])], axis=1)

    def stat_copy(d):
        return pltpu.make_async_remote_copy(
            src_ref=stats.at[c],
            dst_ref=stats.at[c],
            send_sem=ss.at[d],
            recv_sem=sr.at[d],
            device_id=(r, (c + d) % cols),
            device_id_type=MESH,
        )

    def send_stats(d, carry):
        stat_copy(d).start()
        return carry

    lax.fori_loop(1, cols, send_stats, 0)

    def half_copy(i):
        return pltpu.make_async_remote_copy(
            src_ref=x_out.at[i],
            dst_ref=x_in.at[i],
            send_sem=hs.at[i],
            recv_sem=hr.at[i],
            device_id=half_peer,
            device_id_type=MESH,
        )

    inverse = 1.0 / total[...]
    total[...] = inverse
    per_half = half_width // WIDE

    def partial(i, carry):
        columns = pl.ds(pl.multiple_of((i % per_half) * WIDE, WIDE), WIDE)
        value = jnp.dot(
            weights[...], gathered[i // per_half, :, columns], preferred_element_type=F32
        )
        scale = total[...]
        value = value * jnp.concatenate([scale, scale], axis=1)
        low, high = value[:n_half], value[n_half:]
        x_out[i] = jnp.where(xl == 0, high, low).astype(BF16)
        half_copy(i).start()
        own_part[i] = jnp.where(xl == 0, low, high)
        return carry

    lax.fori_loop(0, n_wide, partial, 0)

    def wait_stats(d, carry):
        pltpu.make_async_remote_copy(
            src_ref=stats.at[c],
            dst_ref=stats.at[(c + cols - d) % cols],
            send_sem=ss.at[d],
            recv_sem=sr.at[d],
            device_id=(r, (c + d) % cols),
            device_id_type=MESH,
        ).wait_recv()
        return carry

    lax.fori_loop(1, cols, wait_stats, 0)
    all_peak = stats[0][:, :n_img]
    for i in range(1, cols):
        all_peak = jnp.maximum(all_peak, stats[i][:, :n_img])

    def portion(value):
        return value[:, n_img:] * jnp.exp2((value[:, :n_img] - all_peak) * factor2)

    all_total = portion(stats[0])
    for i in range(1, cols):
        all_total = all_total + portion(stats[i])
    share_me[...] = to_spread(portion(stats[c]) / all_total)
    share_peer[...] = to_spread(portion(stats[half_peer[1]]) / all_total)
    logs[...] = to_spread(all_peak * factor + jnp.log(all_total))

    half_rows = pl.ds(pl.multiple_of(xl * n_half, 8), n_half)

    def z_copy(i, d):
        return pltpu.make_async_remote_copy(
            src_ref=z_out.at[i, d],
            dst_ref=z_in.at[i, d],
            send_sem=zs.at[i, d],
            recv_sem=zr.at[i, d],
            device_id=(r, xl * n_z + (z + d) % n_z),
            device_id_type=MESH,
        )

    def join(i, carry):
        half_copy(i).wait_recv()
        me, peer = share_me[half_rows, :], share_peer[half_rows, :]
        pair_sum[i] = own_part[i] * jnp.concatenate([me, me], axis=1) + x_in[i].astype(
            F32
        ) * jnp.concatenate([peer, peer], axis=1)
        for d in sorted(range(1, n_z), key=lambda d: -min(d, n_z - d)):
            piece = pair_sum[i, pl.ds(pl.multiple_of(((z + d) % n_z) * own, 8), own), :]
            z_out[i, d] = jnp.concatenate([piece[:, :LANES], piece[:, LANES:]], axis=0).astype(BF16)
            z_copy(i, d).start()
        return carry

    relay_paired()
    lax.fori_loop(0, n_wide, join, 0)

    for piece in start:
        copy_of(piece).wait_send()
    for _, _, then in order:
        for piece in then:
            copy_of(piece).wait_send()
    for g in range(n_y):
        core_copy(g).wait_send()
        pair_copies(g, lambda copy: copy.wait_send())

    @pl.when(near_side)
    def _():
        relay_copy(relay).wait_send()

    def wait_stat_sends(d, carry):
        stat_copy(d).wait_send()
        return carry

    lax.fori_loop(1, cols, wait_stat_sends, 0)

    @pl.when(jnp.logical_not(fixed))
    def _():
        relay_copy(pair_in).wait_recv()

    @pl.when(fixed)
    def _():
        take = pltpu.make_async_copy(held_place(held_image), pair_in, paired_sem.at[3])
        take.start()
        take.wait()

    block_in = pair_in[...].astype(F32)
    paired[...] = jnp.concatenate([block_in[:own], block_in[own:]], axis=1)
    near = images[pl.ds(pl.multiple_of(16 * ((own * c) // 16), 16), own + 8), :].astype(F32)
    near = jnp.where((own * c) % 16 == 0, near[:own], near[8:])
    positive = jnp.sum(near * paired[...], axis=1, keepdims=True) * factor
    own_logs = logs[pl.ds(pl.multiple_of(c * own, 8), own), :]
    loss_ref[...] = to_row(own_logs - positive)

    def finish(i, carry):
        value = pair_sum[i, pl.ds(pl.multiple_of(z * own, 8), own), :]
        for d in range(1, n_z):
            z_copy(i, d).wait_recv()
            piece = z_in[i, d].astype(F32)
            value = value + jnp.concatenate([piece[:own], piece[own:]], axis=1)
        columns = pl.ds(pl.multiple_of(i * WIDE, WIDE), WIDE)
        grad_ref[:, columns] = value - paired[:, columns]
        half_copy(i).wait_send()
        for d in range(1, n_z):
            z_copy(i, d).wait_send()
        return carry

    lax.fori_loop(0, n_wide, finish, 0)


def per_device(n_xh, n_xl, text_step, images, texts, logit_scale):
    own, width = texts.shape
    rows, cols = lax.axis_size("row"), lax.axis_size("col")
    n_y = rows // (2 * n_xh)
    n_z = cols // n_xl
    n_img = images.shape[0]
    n_text = rows * own
    n_wide = width // WIDE
    shape = (n_y, n_xh, n_xl, n_z, width, own, text_step)
    dma = pltpu.SemaphoreType.DMA
    vmem = pltpu.VMEM
    loss, grad = pl.pallas_call(
        functools.partial(kernel, shape),
        out_shape=(
            jax.ShapeDtypeStruct((1, own), F32),
            jax.ShapeDtypeStruct((own, width), F32),
        ),
        in_specs=[
            pl.BlockSpec(memory_space=pl.ANY),
            pl.BlockSpec(memory_space=pl.ANY),
            pl.BlockSpec(memory_space=pltpu.SMEM),
        ],
        out_specs=(
            pl.BlockSpec(memory_space=pltpu.VMEM),
            pl.BlockSpec(memory_space=pltpu.VMEM),
        ),
        scratch_shapes=[
            vmem((n_img, width), BF16),
            vmem((own, width), BF16),
            vmem((2 * own, width // 2), BF16),
            vmem((2 * own, width // 2), BF16),
            vmem((own, width), F32),
            vmem((2, n_text, width // 2), BF16),
            vmem((2, n_text, width // 2), BF16),
            vmem((n_img, n_text), F32),
            vmem((n_img, n_text), BF16),
            vmem((n_img, LANES), F32),
            vmem((n_img, LANES), F32),
            vmem((cols, 1, 2 * n_img), F32),
            vmem((n_img, LANES), F32),
            vmem((n_img, LANES), F32),
            vmem((n_img, LANES), F32),
            vmem((n_wide, n_img // 2, WIDE), F32),
            vmem((n_wide, n_img // 2, WIDE), BF16),
            vmem((n_wide, n_img // 2, WIDE), BF16),
            vmem((n_wide, n_img // 2, WIDE), F32),
            vmem((n_wide, n_z, 2 * own, WIDE // 2), BF16),
            vmem((n_wide, n_z, 2 * own, WIDE // 2), BF16),
            dma((2,)),
            dma((4,)),
            dma((n_y, n_xh)),
            dma((1 + n_y, 4)),
            dma((1 + n_y, 4)),
            dma((2, n_y // 2, n_xh)),
            dma((2, n_y // 2, n_xh)),
            dma((2, n_y // 2)),
            dma((2, n_y // 2)),
            dma((n_y,)),
            dma((n_y,)),
            dma((cols,)),
            dma((cols,)),
            dma((n_wide,)),
            dma((n_wide,)),
            dma((n_wide, n_z)),
            dma((n_wide, n_z)),
        ],
        compiler_params=pltpu.CompilerParams(
            collective_id=0, has_side_effects=True, vmem_limit_bytes=60 * 1024 * 1024
        ),
        cost_estimate=pl.CostEstimate(
            flops=4 * n_img * n_text * width,
            bytes_accessed=2 * n_img * width,
            transcendentals=n_img * n_text,
        ),
    )(images, texts, logit_scale)
    return loss.reshape(own), grad


def solution(mesh, n_xh=4, n_xl=2, text_step=256):
    placed = (
        PartitionSpec("row", None),
        PartitionSpec(("col", "row"), None),
        PartitionSpec(),
    )
    return jax.shard_map(
        functools.partial(per_device, n_xh, n_xl, text_step),
        mesh=mesh,
        in_specs=placed,
        out_specs=(PartitionSpec(("row", "col")), PartitionSpec(("row", "col"), None)),
        check_vma=False,
    )
```
